256 devices in a mesh: dp: 8 (over z), vocab: 32 (over x, y, core).
Axes of the slice: x: 4, y: 4, z: 8, core: 2. Of those that a mesh axis runs over, the one named last changes fastest.
Arguments:
- hidden_ref: bfloat16 [512, 8192], P(('dp', 'vocab'))
- head: bfloat16 [8192, 128256], P(None, ('dp', 'vocab'))
- targets: int32 [512], P(('dp', 'vocab')), may hold values from 0 to 128255
- train_loss: float32 [512], P('dp'), may hold values from 9 to 16
- keep_index: int32 [8, 48], P('dp'), may hold values from -1 to 63, as said below
- layer_input: bfloat16 [512, 8192], P('dp', 'vocab'), may hold values from -6 to 6
- cotangent: bfloat16 [512, 8192], P('dp', 'vocab'), may hold values from -0.59765625 to 0.59765625
- layer_weight: bfloat16 [8192, 8192], P('dp', 'vocab'), may hold values from -0.0625 to 0.0625
Outputs:
- excess: float32 [512], P('dp')
- grad_weight: float32 [8192, 8192], P('dp', 'vocab')
- grad_input: bfloat16 [512, 8192], P('dp', 'vocab')
The draws below stay inside these ranges and needn't reach their ends.
Inputs may be any that keep to these rules, and one draw needn't show every extreme that they name: `keep_index`: each group's kept rows are distinct and ascending, all -1 entries stand after them; every group keeps 48 // 2 or more, and in every draw some group keeps all 48.
All inputs are finite; a program needn't handle non-finite values.
Results may differ from the reference program's by a relative error of at most 0.017.
Values may be sent and summed in bfloat16 or wider, within the bound.
No kernel may reach another device: no remote copies, remote signals or barrier semaphores. Data moves between devices by JAX's collectives and lax.ppermute only.
A program may use at most 128 MiB of HBM per device.

```python
import math
import jax
import jax.numpy as jnp
import numpy as np
from jax import lax

D = 8192
VOCAB = 128256
TOK_DP = 64
TOKENS = 512
SLOTS = 48
DV = 256
N_DP = 8
N_VOCAB = 32


def base_hidden(key):
    return jax.random.normal(key, (TOKENS, D), jnp.float32)


def draw_hidden_ref(key, part):
    return base_hidden(key).astype(jnp.bfloat16)


def draw_head(key, part):
    key = jax.random.fold_in(key, 7)
    main_key = jax.random.fold_in(key, 0)
    weights = jax.random.normal(main_key, (D, VOCAB), jnp.float32) * D ** (-0.5)
    return weights.astype(jnp.bfloat16)


def draw_keep_index(key, part):
    key = jax.random.fold_in(key, 11)
    count_key, full_key, order_key = jax.random.split(key, 3)
    counts = jax.random.randint(count_key, (N_DP,), SLOTS // 2, SLOTS + 1)
    fullest = jax.random.randint(full_key, (), 0, N_DP)
    counts = jnp.where(jnp.arange(N_DP) == fullest, SLOTS, counts)
    slot = jnp.arange(SLOTS)[None, :]

    def pick(group_key):
        return jax.random.permutation(group_key, TOK_DP)[:SLOTS]
    chosen = jax.vmap(pick)(jax.random.split(order_key, N_DP))
    chosen = jnp.where(slot < counts[:, None], chosen, TOK_DP)
    chosen = jnp.sort(chosen, axis=1)
    return jnp.where(chosen == TOK_DP, -1, chosen).astype(jnp.int32)


def with_ends(result, stream_key, smallest, largest):
    longest = result.shape.index(max(result.shape))
    spots = []
    for shift in (0, 1):
        where = [jax.random.randint(jax.random.fold_in(stream_key, axis), (), 0, length) for axis, length in enumerate(result.shape)]
        where[longest] = (where[longest] + shift) % result.shape[longest]
        spots.append(tuple(where))
    return result.at[spots[0]].set(smallest).at[spots[1]].set(largest)


def shard_levels(key, shape, cuts, low, largest):
    factor_of, own = 1.0, jax.random.fold_in(key, 6)
    for dim, shards_of in cuts:
        draws = jnp.exp(jax.random.uniform(jax.random.fold_in(own, dim), (shards_of,), jnp.float32, low / len(cuts), largest / len(cuts)))
        factor_of = factor_of * jnp.repeat(draws, shape[dim] // shards_of).reshape([-1 if axis == dim else 1 for axis in range(len(shape))])
    return factor_of


def wide_ids(stream_key, extent, amount, skew):
    portions = [min(1 << octave, amount + 1 - (1 << octave)) * (1 << 20) // math.isqrt((1 << octave) ** skew) + 1 for octave in range((amount + 1).bit_length()) if 1 << octave <= amount]
    scale = 1 + sum(portions) // (1 << 30)
    table = np.cumsum(np.array([max(1, weight // scale) for weight in portions]))
    ticket = jax.random.randint(jax.random.fold_in(stream_key, 1), extent, 0, int(table[len(portions) - 1]))
    start = jnp.left_shift(1, jnp.searchsorted(jnp.asarray(table, jnp.int32), ticket, side="right").astype(jnp.int32))
    rank = start - 1 + jax.random.randint(jax.random.fold_in(stream_key, 4), extent, 0, 1 << 30) % jnp.minimum(start, amount + 1 - start)
    return jax.random.permutation(jax.random.fold_in(stream_key, 2), amount)[rank].astype(jnp.int32)


def noise(stream_key, dims, scale, limit, shards=(), kind=jnp.bfloat16):
    level = shard_levels(stream_key, dims, shards, -0.22, 0.18) if shards else 1.0
    entries = jax.random.normal(stream_key, dims, jnp.float32) * scale * level
    return jnp.minimum(jnp.maximum(entries, -limit), limit).astype(kind)


def setup_inputs(seed: int = 0) -> dict:
    keys = jax.random.split(jax.random.key(seed), 9)
    hidden_ref = draw_hidden_ref(jax.random.fold_in(keys[8], 71), 0)
    head = draw_head(jax.random.fold_in(keys[8], 71), 0)
    targets = with_ends(wide_ids(keys[2], (TOKENS,), VOCAB, 2), jax.random.fold_in(keys[2], 3), 0, VOCAB - 1).astype(jnp.int32)
    train_loss = jnp.clip(9.0 + 7.0 * jax.random.uniform(keys[3], (TOKENS,), jnp.float32) ** shard_levels(keys[3], (TOKENS,), ((0, 8),), -0.2, 0.2), 9.0, 16.0)
    keep_index = draw_keep_index(jax.random.fold_in(keys[8], 71), 0)
    layer_input = noise(keys[5], (TOKENS, D), 1.0, 6.0, ((0, 8), (1, 32)))
    cotangent = noise(keys[6], (TOKENS, D), 0.1, 0.59765625, ((0, 8), (1, 32)))
    layer_weight = noise(keys[7], (D, D), D ** -0.5, 0.0625, ((0, 8), (1, 32)))
    return {"hidden_ref": hidden_ref, "head": head, "targets": targets, "train_loss": train_loss, "keep_index": keep_index, "layer_input": layer_input, "cotangent": cotangent, "layer_weight": layer_weight}


def derivative(values):
    sig = jax.nn.sigmoid(values)
    return sig * (1.0 + values * (1.0 - sig))


def reference(hidden_ref, head, targets, train_loss, keep_index, layer_input, cotangent, layer_weight):
    width = VOCAB // (N_DP * N_VOCAB)

    def block_stats(index):
        columns = lax.dynamic_slice_in_dim(head, index * width, width, 1)
        logits = jnp.dot(hidden_ref, columns, preferred_element_type=jnp.float32)
        top = jnp.max(logits, axis=1)
        total = jnp.sum(jnp.exp(logits - top[:, None]), axis=1)
        ids = index * width + jnp.arange(width, dtype=jnp.int32)
        picked = jnp.sum(jnp.where(targets[:, None] == ids[None, :], logits, jnp.zeros((), logits.dtype)), axis=1)
        return top, total, picked

    tops, totals, pickeds = lax.map(block_stats, jnp.arange(N_DP * N_VOCAB, dtype=jnp.int32))
    top = jnp.max(tops, axis=0)
    total = jnp.sum(totals * jnp.exp(tops - top[None, :]), axis=0)
    ref_loss = top + jnp.log(total) - jnp.sum(pickeds, axis=0)
    excess = train_loss - ref_loss

    valid = keep_index >= 0
    rows = (jnp.arange(N_DP, dtype=jnp.int32)[:, None] * TOK_DP + jnp.where(valid, keep_index, 0).astype(jnp.int32)).reshape(-1)
    valid = valid.reshape(-1)
    credit = jnp.where(valid, jax.nn.softplus(excess[rows]), jnp.zeros((), excess.dtype))
    weight = credit / (jnp.sum(credit) / jnp.sum(valid.astype(jnp.float32)))
    inputs = jnp.where(valid[:, None], layer_input[rows], jnp.zeros((), layer_input.dtype))
    dy = weight[:, None] * cotangent[rows].astype(jnp.float32)
    pre = jnp.dot(inputs, layer_weight, preferred_element_type=jnp.float32)
    slope = (dy * derivative(pre)).astype(jnp.bfloat16)
    grad_weight = jnp.dot(inputs.T, slope, preferred_element_type=jnp.float32)

    def add_block(index, acc):
        part = lax.dynamic_slice_in_dim(slope, index * DV, DV, 1)
        wpart = lax.dynamic_slice_in_dim(layer_weight, index * DV, DV, 1)
        term = lax.dot_general(part, wpart, (((1,), (1,)), ((), ())), preferred_element_type=jnp.float32)
        term = lax.optimization_barrier(term.astype(jnp.bfloat16))
        return acc + term.astype(jnp.float32)

    back = lax.fori_loop(0, N_VOCAB, add_block, jnp.zeros((rows.shape[0], D), jnp.float32))
    grad_rows = jnp.where(valid[:, None], dy + back, jnp.zeros((), dy.dtype))
    grad_input = jnp.zeros((TOKENS, D), jnp.float32).at[rows].add(grad_rows).astype(jnp.bfloat16)
    return excess, grad_weight, grad_input
```

```python
import jax
import jax.numpy as jnp
from jax import lax
from jax.sharding import PartitionSpec as P

AXES = ("dp", "vocab")
NZ, NX, NY, NC = 8, 4, 4, 2
STRIDE = {"z": 32, "x": 8, "y": 2, "c": 1}
SIZE = {"z": NZ, "x": NX, "y": NY, "c": NC}
BF = jnp.bfloat16
F32 = jnp.float32


def coords():
    v = lax.axis_index("vocab")
    return {"z": lax.axis_index("dp"), "x": v // 8, "y": (v // 2) % 4, "c": v % 2}


def ex(a, axis, mask):
    m = STRIDE[axis] * mask
    return lax.ppermute(a, AXES, [(i, i ^ m) for i in range(256)])


def shift(a, axis, k):
    st, n = STRIDE[axis], SIZE[axis]
    pairs = []
    for i in range(256):
        p = (i // st) % n
        pairs.append((i, i + ((p + k) % n - p) * st))
    return lax.ppermute(a, AXES, pairs)


def bit(co, axis, b):
    return ((co[axis] >> b) & 1) == 1


def pair_up(mine, other, hi, dim):
    return jnp.where(hi, jnp.concatenate([other, mine], dim), jnp.concatenate([mine, other], dim))


def gather_xor(a, co, axis, dim):
    for b in range(SIZE[axis].bit_length() - 1):
        a = pair_up(a, ex(a, axis, 1 << b), bit(co, axis, b), dim)
    return a


def gather_ring(a, co, axis, dim, cut):
    n = SIZE[axis]
    me = co[axis]
    shape = a.shape[:dim] + (n,) + a.shape[dim:]
    buf = jnp.zeros(shape, a.dtype)

    def put(buf, block, pos, col=0):
        block = jnp.expand_dims(block, dim)
        start = [0] * len(shape)
        start[dim] = pos % n
        start[-1] = col
        return lax.dynamic_update_slice(buf, block, tuple(jnp.int32(s) for s in start))

    buf = put(buf, a, me)
    up, down = a, a
    for k in range(1, n // 2):
        up = shift(up, axis, 1)
        down = shift(down, axis, -1)
        buf = put(buf, up, me - k + n)
        buf = put(buf, down, me + k)
    left = shift(up[..., :cut], axis, 1)
    right = shift(down[..., cut:], axis, -1)
    buf = put(buf, left, me + n // 2)
    buf = put(buf, right, me + n // 2, cut)
    return buf


def halve(a, co, axis, b, dim, dtype):
    hi = bit(co, axis, b)
    first = lax.index_in_dim(a, 0, dim, keepdims=False)
    second = lax.index_in_dim(a, 1, dim, keepdims=False)
    keep = jnp.where(hi, second, first)
    send = jnp.where(hi, first, second).astype(dtype)
    return keep.astype(F32) + ex(send, axis, 1 << b).astype(F32)


def derivative(values):
    sig = jax.nn.sigmoid(values)
    return sig * (1.0 + values * (1.0 - sig))


def transpose_pairs(back):
    pairs = []
    for g in range(8):
        for v in range(32):
            src, dst = g * 32 + v, (v // 4) * 32 + 4 * g + v % 4
            pairs.append((dst, src) if back else (src, dst))
    return pairs


def block_stats(logits, labels, first):
    ids = first + jnp.arange(logits.shape[1], dtype=jnp.int32)
    top = jnp.max(logits, axis=1)
    picked = jnp.sum(jnp.where(labels[:, None] == ids[None, :], logits, 0.0), axis=1)
    return top, picked


def on_device(
    hidden_ref, head, targets, train_loss, keep_index, layer_input, cotangent, layer_weight
):
    co = coords()
    voc_dev = head.shape[1]
    d = head.shape[0]
    dv = layer_weight.shape[1]
    slots = keep_index.shape[1]
    rows = train_loss.shape[0]
    shard = lax.axis_index("dp") * 32 + lax.axis_index("vocab")

    other_head = ex(head, "c", 1)

    cut = (d // 128 // 2) * 128
    p = hidden_ref[None, :, :cut]
    q = hidden_ref[None, :, cut:]
    p = gather_xor(p, co, "y", 0)
    p = gather_xor(p, co, "x", 0)
    q = gather_xor(q, co, "z", 0)
    p = p.reshape(32, cut)
    p = gather_ring(p, co, "z", 0, cut // 2).reshape(256, cut)
    q = q.reshape(8, 2, d - cut)
    q = gather_ring(q, co, "y", 1, cut // 2).reshape(8, 8, d - cut)
    q = gather_ring(q, co, "x", 1, cut // 2).reshape(256, d - cut)

    kept = keep_index[0]
    labels = targets.astype(F32)[None]
    labels = gather_xor(gather_xor(labels, co, "y", 0), co, "x", 0).reshape(32)
    meta = jnp.concatenate([train_loss, kept.astype(F32), labels])[None]
    meta = gather_xor(meta, co, "z", 0)
    all_loss = meta[:, :rows]
    all_kept = meta[:, rows : rows + slots].astype(jnp.int32)
    labels = meta[:, rows + slots :].reshape(256).astype(jnp.int32)

    valid = kept >= 0
    chosen = jnp.where(valid, kept, 0)
    inputs = jnp.where(
        valid[:, None], jnp.take(layer_input, chosen, axis=0), jnp.zeros((), layer_input.dtype)
    )
    cot = jnp.take(cotangent, chosen, axis=0).astype(F32)
    xs = lax.ppermute(inputs, AXES, transpose_pairs(False))[None]
    xs = gather_xor(gather_xor(xs, co, "y", 0), co, "x", 0)
    xs = xs.reshape(8, 2, 1, slots, dv)
    xs = pair_up(xs, ex(xs, "c", 1), bit(co, "c", 0), 2)
    xs = xs.reshape(8, 4, slots, dv)
    x_all = jnp.swapaxes(xs, 1, 2).reshape(8 * slots, 4 * dv)
    pre = jnp.dot(x_all, layer_weight, preferred_element_type=F32)
    pre = pre.reshape(2, 2, 2, slots, dv)
    pre = halve(pre, co, "z", 0, 2, F32)
    pre = halve(pre, co, "z", 1, 1, F32)
    pre = halve(pre, co, "z", 2, 0, F32)
    u = (cot * derivative(pre)).astype(BF)[None, None, None]
    u = pair_up(u, ex(u, "z", 4), bit(co, "z", 2), 0)
    u = pair_up(u, ex(u, "z", 2), bit(co, "z", 1), 1)
    u = pair_up(u, ex(u, "z", 1), bit(co, "z", 0), 2)
    u_all = u.reshape(8 * slots, dv)
    terms = lax.dot_general(
        u_all, layer_weight, (((1,), (1,)), ((), ())), preferred_element_type=F32
    ).astype(BF)
    terms = terms.reshape(8, slots, 4, dv).swapaxes(1, 2).reshape(2, 2, 2, 2, 2, slots, dv)
    back = halve(terms, co, "c", 0, 4, BF).astype(BF)
    back = halve(back, co, "y", 0, 3, BF).astype(BF)
    back = halve(back, co, "y", 1, 2, BF)
    back = halve(back, co, "x", 0, 1, F32)
    back = halve(back, co, "x", 1, 0, F32)
    back = lax.ppermute(back, AXES, transpose_pairs(True))
    spread = (jnp.arange(rows, dtype=jnp.int32)[:, None] == kept[None, :]).astype(F32)
    back = jnp.dot(spread, back, precision=lax.Precision.HIGHEST, preferred_element_type=F32)
    mine_grad = cotangent.astype(F32) + back

    def logits_of(w):
        return jnp.dot(p, w[:cut], preferred_element_type=F32) + jnp.dot(
            q, w[cut:], preferred_element_type=F32
        )

    one, two = logits_of(head), logits_of(other_head)
    top1, pick1 = block_stats(one, labels, shard * voc_dev)
    top2, pick2 = block_stats(two, labels, (shard ^ 1) * voc_dev)
    top = jnp.maximum(top1, top2)
    total = jnp.sum(jnp.exp(one - top[:, None]), axis=1) + jnp.sum(
        jnp.exp(two - top[:, None]), axis=1
    )
    stats = jnp.stack([top, total, pick1 + pick2])
    for axis, mask in (("y", 1), ("y", 2), ("x", 1), ("x", 2), ("z", 1), ("z", 2), ("z", 4)):
        got = ex(stats, axis, mask)
        top = jnp.maximum(stats[0], got[0])
        total = stats[1] * jnp.exp(stats[0] - top) + got[1] * jnp.exp(got[0] - top)
        stats = jnp.stack([top, total, stats[2] + got[2]])
    ref_loss = (stats[0] + jnp.log(stats[1]) - stats[2]).reshape(8, 16, 1, 2)
    ref_loss = pair_up(ref_loss, ex(ref_loss, "c", 1), bit(co, "c", 0), 2).reshape(8, rows)
    excess = all_loss - ref_loss

    hot = all_kept[:, :, None] == jnp.arange(rows, dtype=jnp.int32)[None, None, :]
    is_kept = jnp.any(hot, axis=1)
    credit = jnp.where(is_kept, jax.nn.softplus(excess), 0.0)
    weight = credit / (jnp.sum(credit) / jnp.sum(is_kept.astype(F32)))
    slot_weight = jnp.sum(jnp.where(hot, weight[:, None, :], 0.0), axis=2).reshape(8 * slots)
    slope = (slot_weight[:, None] * u_all.astype(F32)).astype(BF)
    grad_weight = lax.dot_general(
        x_all, slope, (((0,), (0,)), ((), ())), preferred_element_type=F32
    )
    own_weight = lax.dynamic_index_in_dim(weight, co["z"], 0, keepdims=False)
    own_excess = lax.dynamic_index_in_dim(excess, co["z"], 0, keepdims=False)
    grad_input = (own_weight[:, None] * mine_grad).astype(BF)
    return (own_excess, grad_weight, grad_input)


def solution(mesh):
    in_specs = (
        P(("dp", "vocab"), None),
        P(None, ("dp", "vocab")),
        P(("dp", "vocab")),
        P("dp"),
        P("dp", None),
        P("dp", "vocab"),
        P("dp", "vocab"),
        P("dp", "vocab"),
    )
    out_specs = (P("dp"), P("dp", "vocab"), P("dp", "vocab"))
    return jax.shard_map(
        on_device, mesh=mesh, in_specs=in_specs, out_specs=out_specs, check_vma=False
    )
```

```python
import functools

import jax
import jax.numpy as jnp
from jax import lax
from jax.experimental import pallas as pl
from jax.experimental.pallas import tpu as pltpu
from jax.sharding import PartitionSpec as P

AXES = ("dp", "vocab")
NZ, NX, NY, NC = 8, 4, 4, 2
STRIDE = {"z": 32, "x": 8, "y": 2, "c": 1}
SIZE = {"z": NZ, "x": NX, "y": NY, "c": NC}
BF = jnp.bfloat16
F32 = jnp.float32


def coords():
    v = lax.axis_index("vocab")
    return {"z": lax.axis_index("dp"), "x": v // 8, "y": (v // 2) % 4, "c": v % 2}


def ex(a, axis, mask):
    m = STRIDE[axis] * mask
    return lax.ppermute(a, AXES, [(i, i ^ m) for i in range(256)])


def shift(a, axis, k):
    st, n = STRIDE[axis], SIZE[axis]
    pairs = []
    for i in range(256):
        p = (i // st) % n
        pairs.append((i, i + ((p + k) % n - p) * st))
    return lax.ppermute(a, AXES, pairs)


def bit(co, axis, b):
    return ((co[axis] >> b) & 1) == 1


def pair_up(mine, other, hi, dim):
    return jnp.where(hi, jnp.concatenate([other, mine], dim), jnp.concatenate([mine, other], dim))


def gather_xor(a, co, axis, dim):
    for b in range(SIZE[axis].bit_length() - 1):
        a = pair_up(a, ex(a, axis, 1 << b), bit(co, axis, b), dim)
    return a


def gather_ring(a, co, axis, dim, cut):
    me = co[axis]
    shape = a.shape[:dim] + (4,) + a.shape[dim:]
    buf = jnp.zeros(shape, a.dtype)

    def put(buf, block, pos, col=0):
        start = [jnp.int32(0)] * len(shape)
        start[dim] = pos % 4
        start[-1] = jnp.int32(col)
        return lax.dynamic_update_slice(buf, jnp.expand_dims(block, dim), tuple(start))

    up, down = shift(a, axis, 1), shift(a, axis, -1)
    left = shift(up[..., :cut], axis, 1)
    right = shift(down[..., cut:], axis, -1)
    buf = put(buf, a, me)
    buf = put(buf, up, me + 3)
    buf = put(buf, down, me + 1)
    buf = put(buf, left, me + 2)
    return put(buf, right, me + 2, cut)


def halve(a, co, axis, b, dim, dtype):
    hi = bit(co, axis, b)
    first = lax.index_in_dim(a, 0, dim, keepdims=False)
    second = lax.index_in_dim(a, 1, dim, keepdims=False)
    keep = jnp.where(hi, second, first)
    send = jnp.where(hi, first, second).astype(dtype)
    return keep.astype(F32) + ex(send, axis, 1 << b).astype(F32)


def derivative(values):
    sig = jax.nn.sigmoid(values)
    return sig * (1.0 + values * (1.0 - sig))


def transpose_pairs(back):
    pairs = []
    for g in range(8):
        for v in range(32):
            src, dst = g * 32 + v, (v // 4) * 32 + 4 * g + v % 4
            pairs.append((dst, src) if back else (src, dst))
    return pairs


def split3(values):
    one = lax.reduce_precision(values, 8, 7)
    two = lax.reduce_precision(values - one, 8, 7)
    return [one, two, values - one - two]


def logits_kernel(steps, first_ref, p_ref, q_ref, meta_ref, one_ref, two_ref, out_ref, acc1, acc2):
    k = pl.program_id(0)

    @pl.when(k == 0)
    def _():
        acc1[...] = jnp.zeros_like(acc1)
        acc2[...] = jnp.zeros_like(acc2)

    def add(a):
        acc1[...] += jnp.dot(a, one_ref[...], preferred_element_type=F32)
        acc2[...] += jnp.dot(a, two_ref[...], preferred_element_type=F32)

    @pl.when(k < steps)
    def _():
        add(p_ref[...])

    @pl.when(k >= steps)
    def _():
        add(q_ref[...])

    @pl.when(k == 2 * steps - 1)
    def _():
        meta = meta_ref[...].astype(F32)
        label = (meta[:, 0:1] * 65536.0 + meta[:, 1:2] * 256.0 + meta[:, 2:3]).astype(jnp.int32)
        loss = meta[:, 3:4] + meta[:, 4:5] + meta[:, 5:6]
        one, two = acc1[...], acc2[...]
        top = jnp.maximum(
            jnp.max(one, axis=1, keepdims=True), jnp.max(two, axis=1, keepdims=True)
        )
        total = jnp.sum(jnp.exp(one - top), axis=1, keepdims=True) + jnp.sum(
            jnp.exp(two - top), axis=1, keepdims=True
        )
        ids = lax.broadcasted_iota(jnp.int32, one.shape, 1)
        picked = jnp.sum(
            jnp.where(ids == label - first_ref[0], one, 0.0)
            + jnp.where(ids == label - first_ref[1], two, 0.0),
            axis=1,
            keepdims=True,
        )
        lane = lax.broadcasted_iota(jnp.int32, (one.shape[0], 128), 1)
        cols = jnp.zeros(lane.shape, F32)
        for j, col in enumerate((top, total, picked, loss, meta[:, 6:7])):
            cols = jnp.where(lane == j, col, cols)
        out_ref[...] = cols.T[:8]


def local_stats(p, q, head, other_head, first):
    d, voc = head.shape
    rows = p.shape[0]
    kb = min(1024, p.shape[1])
    steps = p.shape[1] // kb
    return pl.pallas_call(
        functools.partial(logits_kernel, steps),
        out_shape=jax.ShapeDtypeStruct((8, rows), F32),
        grid_spec=pltpu.PrefetchScalarGridSpec(
            num_scalar_prefetch=1,
            grid=(2 * steps,),
            in_specs=[
                pl.BlockSpec((rows, kb), lambda k, f: (0, jnp.minimum(k, steps - 1))),
                pl.BlockSpec((rows, kb), lambda k, f: (0, jnp.maximum(k - steps, 0))),
                pl.BlockSpec((rows, 128), lambda k, f: (0, p.shape[1] // 128)),
                pl.BlockSpec((kb, voc), lambda k, f: (k, 0)),
                pl.BlockSpec((kb, voc), lambda k, f: (k, 0)),
            ],
            out_specs=pl.BlockSpec((8, rows), lambda k, f: (0, 0)),
            scratch_shapes=[pltpu.VMEM((rows, voc), F32), pltpu.VMEM((rows, voc), F32)],
        ),
        compiler_params=pltpu.CompilerParams(vmem_limit_bytes=24 * 1024 * 1024),
        cost_estimate=pl.CostEstimate(
            flops=4 * rows * d * voc,
            bytes_accessed=4 * d * voc + 2 * rows * d,
            transcendentals=2 * rows * voc,
        ),
    )(first, p, q, q, head, other_head)


def combine(parts):
    top = functools.reduce(jnp.maximum, [s[0] for s in parts])
    total = sum(s[1] * jnp.exp(s[0] - top) for s in parts)
    return jnp.stack([top, total, sum(s[2] for s in parts)])


def on_device(
    hidden_ref, head, targets, train_loss, keep_index, layer_input, cotangent, layer_weight
):
    co = coords()
    voc_dev = head.shape[1]
    half = head.shape[0] // 2
    dv = layer_weight.shape[1]
    rows = train_loss.shape[0]
    vocab = lax.axis_index("vocab")
    shard = lax.axis_index("dp") * 32 + vocab

    other_head = ex(head, "c", 1)

    mine = vocab * 2 + jnp.arange(2, dtype=jnp.int32)
    is_kept = jnp.any(keep_index[0][None, :] == mine[:, None], axis=1)
    loss = split3(lax.dynamic_slice_in_dim(train_loss, vocab * 2, 2))
    meta = [targets // 65536, (targets // 256) % 256, targets % 256, *loss, is_kept]
    meta = jnp.stack([m.astype(F32) for m in meta], axis=1).astype(BF)
    meta = jnp.pad(meta, ((0, 0), (0, 128 - meta.shape[1])))
    h = jnp.concatenate([hidden_ref, meta], axis=1)[None]
    h = gather_xor(h, co, "z", 0).reshape(16, 2 * half + 128)
    p, q = h[:, :half], h[:, half:]
    p = gather_ring(p, co, "y", 0, half // 2)
    q = gather_ring(q, co, "x", 0, half // 2)
    p = gather_ring(p, co, "x", 0, half // 2).reshape(256, half)
    q = gather_ring(q, co, "y", 1, half // 2).reshape(256, half + 128)

    xs = lax.ppermute(layer_input, AXES, transpose_pairs(False))[None]
    xs = gather_xor(gather_xor(xs, co, "y", 0), co, "x", 0)
    xs = xs.reshape(8, 2, 1, rows, dv)
    xs = pair_up(xs, ex(xs, "c", 1), bit(co, "c", 0), 2)
    xs = xs.reshape(8, 4, rows, dv)
    x_all = jnp.swapaxes(xs, 1, 2).reshape(8 * rows, 4 * dv)
    pre = jnp.dot(x_all, layer_weight, preferred_element_type=F32)
    pre = pre.reshape(2, 2, 2, rows, dv)
    pre = halve(pre, co, "z", 0, 2, BF)
    pre = halve(pre, co, "z", 1, 1, F32)
    pre = halve(pre, co, "z", 2, 0, F32)
    u = (cotangent.astype(F32) * derivative(pre)).astype(BF)[None, None, None]
    u = pair_up(u, ex(u, "z", 4), bit(co, "z", 2), 0)
    u = pair_up(u, ex(u, "z", 2), bit(co, "z", 1), 1)
    u = pair_up(u, ex(u, "z", 1), bit(co, "z", 0), 2)
    u_all = u.reshape(8 * rows, dv)
    terms = lax.dot_general(
        u_all, layer_weight, (((1,), (1,)), ((), ())), preferred_element_type=F32
    ).astype(BF)
    terms = terms.reshape(8, rows, 4, dv).swapaxes(1, 2).reshape(2, 2, 2, 2, 2, rows, dv)
    back = halve(terms, co, "c", 0, 4, BF).astype(BF)
    back = halve(back, co, "y", 0, 3, BF).astype(BF)
    back = halve(back, co, "y", 1, 2, BF)
    back = halve(back, co, "x", 0, 1, F32)
    back = halve(back, co, "x", 1, 0, F32)
    back = lax.ppermute(back, AXES, transpose_pairs(True))
    mine_grad = cotangent.astype(F32) + back

    first = jnp.stack([shard * voc_dev, (shard ^ 1) * voc_dev]).astype(jnp.int32)
    local = local_stats(p, q, head, other_head, first)
    stats = local[:3]
    for axis, masks in (("y", (1, 2, 3)), ("x", (1, 2, 3)), ("z", (1,)), ("z", (2, 4, 6))):
        stats = combine([stats] + [ex(stats, axis, m) for m in masks])
    excess = local[3] - (stats[0] + jnp.log(stats[1]) - stats[2])
    both = jnp.stack([excess, local[4]]).reshape(2, 16, 8, 1, 2)
    both = pair_up(both, ex(both, "c", 1), bit(co, "c", 0), 3)
    both = both.transpose(0, 2, 1, 3, 4).reshape(2, 8, rows)
    excess, kept = both[0], both[1]

    credit = jnp.where(kept > 0.0, jax.nn.softplus(excess), 0.0)
    weight = credit / (jnp.sum(credit) / jnp.sum(kept))
    slope = (weight.reshape(8 * rows)[:, None] * u_all.astype(F32)).astype(BF)
    grad_weight = lax.dot_general(
        x_all, slope, (((0,), (0,)), ((), ())), preferred_element_type=F32
    )
    own_weight = lax.dynamic_index_in_dim(weight, co["z"], 0, keepdims=False)
    own_excess = lax.dynamic_index_in_dim(excess, co["z"], 0, keepdims=False)
    grad_input = (own_weight[:, None] * mine_grad).astype(BF)
    return (own_excess, grad_weight, grad_input)


def solution(mesh):
    in_specs = (
        P(("dp", "vocab"), None),
        P(None, ("dp", "vocab")),
        P(("dp", "vocab")),
        P("dp"),
        P("dp", None),
        P("dp", "vocab"),
        P("dp", "vocab"),
        P("dp", "vocab"),
    )
    out_specs = (P("dp"), P("dp", "vocab"), P("dp", "vocab"))
    return jax.shard_map(
        on_device, mesh=mesh, in_specs=in_specs, out_specs=out_specs, check_vma=False
    )
```

```python
import functools

import jax
import jax.numpy as jnp
from jax import lax
from jax.experimental import pallas as pl
from jax.experimental.pallas import tpu as pltpu
from jax.sharding import PartitionSpec as P

AXES = ("dp", "vocab")
NZ, NX, NY, NC = 8, 4, 4, 2
STRIDE = {"z": 32, "x": 8, "y": 2, "c": 1}
SIZE = {"z": NZ, "x": NX, "y": NY, "c": NC}
BF = jnp.bfloat16
F32 = jnp.float32


def coords():
    v = lax.axis_index("vocab")
    return {"z": lax.axis_index("dp"), "x": v // 8, "y": (v // 2) % 4, "c": v % 2}


def ex(a, axis, mask):
    m = STRIDE[axis] * mask
    return lax.ppermute(a, AXES, [(i, i ^ m) for i in range(256)])


def shift(a, axis, k):
    st, n = STRIDE[axis], SIZE[axis]
    pairs = []
    for i in range(256):
        p = (i // st) % n
        pairs.append((i, i + ((p + k) % n - p) * st))
    return lax.ppermute(a, AXES, pairs)


def bit(co, axis, b):
    return ((co[axis] >> b) & 1) == 1


def pair_up(mine, other, hi, dim):
    return jnp.where(hi, jnp.concatenate([other, mine], dim), jnp.concatenate([mine, other], dim))


def gather_direct(a, co, axis, dim):
    me = co[axis]
    blocks = [(0, a)] + [(k, ex(a, axis, k)) for k in (1, 3, 2)]
    buf = jnp.zeros(a.shape[:dim] + (4,) + a.shape[dim:], a.dtype)
    for k, block in blocks:
        buf = place(buf, block, dim, me ^ k)
    return buf


def place(buf, block, dim, pos, col=0):
    start = [jnp.int32(0)] * buf.ndim
    start[dim] = pos % 4
    start[-1] = jnp.int32(col)
    return lax.dynamic_update_slice(buf, jnp.expand_dims(block, dim), tuple(start))


def ring_first(a, axis):
    return shift(a, axis, 1), shift(a, axis, -1)


def ring_second(up, down, axis, cut):
    return shift(up[..., :cut], axis, 1), shift(down[..., cut:], axis, -1)


def ring_stack(a, near, far, co, axis, dim, cut):
    me = co[axis]
    buf = jnp.zeros(a.shape[:dim] + (4,) + a.shape[dim:], a.dtype)
    buf = place(buf, a, dim, me)
    buf = place(buf, near[0], dim, me + 3)
    buf = place(buf, near[1], dim, me + 1)
    buf = place(buf, far[0], dim, me + 2)
    return place(buf, far[1], dim, me + 2, cut)


def halve(a, co, axis, b, dim, dtype):
    hi = bit(co, axis, b)
    first = lax.index_in_dim(a, 0, dim, keepdims=False)
    second = lax.index_in_dim(a, 1, dim, keepdims=False)
    keep = jnp.where(hi, second, first)
    send = jnp.where(hi, first, second).astype(dtype)
    return keep.astype(F32) + ex(send, axis, 1 << b).astype(F32)


def derivative(values):
    sig = jax.nn.sigmoid(values)
    return sig * (1.0 + values * (1.0 - sig))


def plane_pairs(back):
    pairs = [((v // 4) * 32 + 4 * g + v % 4, g * 32 + v) for g in range(8) for v in range(32)]
    return [(j, i) for i, j in pairs] if back else pairs


def logits_kernel(first_ref, p_ref, q_ref, one_ref, two_ref, out_ref):
    half = p_ref.shape[1]
    dims = (((1,), (1,)), ((), ()))

    def logits(w_ref):
        return lax.dot_general(
            w_ref[:, :half], p_ref[...], dims, preferred_element_type=F32
        ) + lax.dot_general(
            w_ref[:, half:], q_ref[:, :half], dims, preferred_element_type=F32
        )

    meta = q_ref[:, half:].astype(F32).T
    label = (meta[0:1] * 65536.0 + meta[1:2] * 256.0 + meta[2:3]).astype(jnp.int32)
    one, two = logits(one_ref), logits(two_ref)
    top = jnp.maximum(jnp.max(one, axis=0, keepdims=True), jnp.max(two, axis=0, keepdims=True))
    total = jnp.sum(jnp.exp(one - top), axis=0, keepdims=True) + jnp.sum(
        jnp.exp(two - top), axis=0, keepdims=True
    )
    ids = lax.broadcasted_iota(jnp.int32, one.shape, 0)
    picked = jnp.sum(
        jnp.where(ids == label - first_ref[0], one, 0.0)
        + jnp.where(ids == label - first_ref[1], two, 0.0),
        axis=0,
        keepdims=True,
    )
    row = lax.broadcasted_iota(jnp.int32, out_ref.shape, 0)
    out = jnp.zeros(out_ref.shape, F32)
    for j, value in enumerate((top, total, picked)):
        out = jnp.where(row == j, value, out)
    out_ref[...] = out


def local_stats(p, q, head, other_head, first):
    voc, d = head.shape
    rows = p.shape[0]
    return pl.pallas_call(
        logits_kernel,
        out_shape=jax.ShapeDtypeStruct((8, rows), F32),
        in_specs=[pl.BlockSpec(memory_space=pltpu.SMEM)]
        + [pl.BlockSpec(memory_space=pltpu.VMEM)] * 4,
        out_specs=pl.BlockSpec(memory_space=pltpu.VMEM),
        compiler_params=pltpu.CompilerParams(vmem_limit_bytes=30 * 1024 * 1024),
        cost_estimate=pl.CostEstimate(
            flops=4 * rows * d * voc,
            bytes_accessed=4 * d * voc + 2 * rows * d,
            transcendentals=2 * rows * voc,
        ),
    )(first, p, q, head, other_head)


def split3(values):
    one = lax.reduce_precision(values, 8, 7)
    two = lax.reduce_precision(values - one, 8, 7)
    return jnp.concatenate([one, two, values - one - two]).astype(BF)


def swap_both(stats, payload, axis, mask):
    n = stats.shape[0]
    terms = split3(stats)
    terms = jnp.pad(terms, ((0, -terms.shape[0] % 16), (0, 0)))
    got = ex(jnp.concatenate([payload, terms]), axis, mask)
    m = payload.shape[0]
    t = got[m : m + 3 * n].astype(F32)
    return (t[:n] + t[n : 2 * n]) + t[2 * n :], got[:m]


def combine(a, b):
    n = a.shape[0] // 3
    top = jnp.maximum(a[:n], b[:n])
    total = a[n : 2 * n] * jnp.exp(a[:n] - top) + b[n : 2 * n] * jnp.exp(b[:n] - top)
    return jnp.concatenate([top, total, a[2 * n :] + b[2 * n :]])


def split_halves(a, hi):
    n = a.shape[0] // 2
    return jnp.where(hi, a[n:], a[:n]), jnp.where(hi, a[:n], a[n:]).astype(BF)


def sync(*values):
    return lax.optimization_barrier(values)


def columns(a, first, size):
    return lax.slice_in_dim(a, first, first + size, axis=a.ndim - 1)


def on_device(
    hidden_ref, head, targets, train_loss, keep_index, layer_input, cotangent, layer_weight
):
    co = coords()
    voc_dev = head.shape[1]
    half = head.shape[0] // 2
    dv = layer_weight.shape[1]
    rows = train_loss.shape[0]
    vocab = lax.axis_index("vocab")
    shard = lax.axis_index("dp") * 32 + vocab

    head = head.T
    other_head = ex(head, "c", 1)

    def bits(axis, b):
        return bit(co, axis, b)

    lane = lax.broadcasted_iota(jnp.int32, (2, 128), 1)
    t = targets[:, None]
    meta = jnp.where(lane == 0, t // 65536, jnp.where(lane == 1, (t // 256) % 256, t % 256))
    meta = jnp.where(lane < 3, meta, 0).astype(BF)
    h = jnp.concatenate([hidden_ref, meta], axis=1)[None]
    h = pair_up(h, ex(h, "z", 4), bits("z", 2), 0)[:, None]
    xs = lax.ppermute(layer_input, AXES, plane_pairs(False))[None, None]
    h, xs = sync(h, xs)

    h = pair_up(h, ex(h, "z", 2), bits("z", 1), 1)[:, :, None]
    xs = pair_up(xs, ex(xs, "x", 2), bits("x", 1), 0)
    h, xs = sync(h, xs)

    h = pair_up(h, ex(h, "z", 1), bits("z", 0), 2).reshape(16, 2 * half + 128)
    xs = pair_up(xs, ex(xs, "y", 2), bits("y", 1), 1)
    h, xs, other_head = sync(h, xs, other_head)

    p = gather_direct(h[:, :half], co, "y", 0)
    q = gather_direct(h[:, half:], co, "x", 0)
    xs = pair_up(xs, ex(xs, "y", 1), bits("y", 0), 3)[:, None]
    p, q, xs = sync(p, q, xs)

    p_near, q_near = ring_first(p, "x"), ring_first(q, "y")
    xs = pair_up(xs, ex(xs, "x", 1), bits("x", 0), 1).reshape(8 * rows, 2 * dv)
    got = ex(xs, "c", 1)
    low, high = [
        jnp.concatenate([columns(a, 0, dv), columns(b, 0, dv), columns(a, dv, dv), columns(b, dv, dv)], 1)
        for a, b in ((xs, got), (got, xs))
    ]
    x_all = jnp.where(bits("c", 0), high, low)
    pre = jnp.dot(x_all, layer_weight, preferred_element_type=F32)
    p_near, q_near, pre = sync(p_near, q_near, pre)

    p_far, q_far = ring_second(*p_near, "x", half // 2), ring_second(*q_near, "y", half // 2)
    pre = halve(pre.reshape(2, 2, 2, rows, dv), co, "z", 0, 2, BF)
    pre = halve(pre, co, "z", 1, 1, BF).astype(BF).reshape(2 * rows, dv)
    p_far, q_far, pre = sync(p_far, q_far, pre)

    p = ring_stack(p, p_near, p_far, co, "x", 0, half // 2).reshape(256, half)
    q = ring_stack(q, q_near, q_far, co, "y", 1, half // 2).reshape(256, half + 128)
    first = jnp.stack([shard * voc_dev, (shard ^ 1) * voc_dev]).astype(jnp.int32)
    stats = local_stats(p, q, head, other_head, first)[:3]

    here = jnp.arange(8, dtype=jnp.int32) == co["z"]
    marks = jnp.any(keep_index[0][None, :] == jnp.arange(rows, dtype=jnp.int32)[:, None], axis=1)
    own = jnp.stack([train_loss, marks.astype(F32)]).reshape(2, 16, 1, 2, 2)
    own = jnp.where(bits("c", 0), own[:, :, :, 1], own[:, :, :, 0])
    own = jnp.where(here[None, None, :, None], own, 0.0).reshape(2, 256)

    got = ex(jnp.concatenate([pre, cotangent]), "z", 4)
    pre = pre.astype(F32) + got[: 2 * rows].astype(F32)
    cot = pair_up(cotangent, got[2 * rows :], bits("z", 2), 0)
    u = (cot.astype(F32) * derivative(pre)).astype(BF)
    got_s = ex(jnp.concatenate([stats, own]), "z", 4)
    stats, own = combine(stats, got_s[:3]), own + got_s[3:]

    got_s, got = swap_both(jnp.concatenate([stats, own]), u, "z", 2)
    stats, own = combine(stats, got_s[:3]), own + got_s[3:]
    u = pair_up(u.reshape(2, 1, rows, dv), got.reshape(2, 1, rows, dv), bits("z", 1), 1)

    u = u.reshape(4 * rows, dv)
    got_s, got = swap_both(jnp.concatenate([stats, own]), u, "z", 1)
    stats, own = combine(stats, got_s[:3]), own + got_s[3:]
    u = pair_up(u.reshape(4, 1, rows, dv), got.reshape(4, 1, rows, dv), bits("z", 0), 1)
    u_all = u.reshape(8 * rows, dv)

    terms = lax.dot_general(
        u_all, layer_weight, (((1,), (1,)), ((), ())), preferred_element_type=F32
    ).astype(BF)
    back = jnp.concatenate([columns(terms, j * dv, dv) for j in (0, 2, 1, 3)])
    keep, send = split_halves(back, bits("c", 0))
    got_s, got = swap_both(jnp.concatenate([stats, own]), send, "c", 1)
    hi = bits("c", 0)
    both = [jnp.where(hi, jnp.stack([b, a], 1), jnp.stack([a, b], 1)) for a, b in ((stats, got_s[:3]), (own, got_s[3:]))]
    stats, own = both[0].reshape(6, 256), both[1].reshape(4, 256)

    back = (keep.astype(F32) + got.astype(F32)).astype(BF)
    for axis, mask in (("y", 1), ("x", 1), ("y", 2)):
        hi = bits(axis, mask // 2)
        if axis == "x":
            back = back.reshape(2, 2, 2 * rows, dv).swapaxes(0, 1).reshape(8 * rows, dv)
        elif mask == 2:
            back = back.reshape(2, 2, rows, dv).swapaxes(0, 1).reshape(4 * rows, dv)
        keep, send = split_halves(back, hi)
        got_s, got = swap_both(stats, send, axis, mask)
        stats = combine(stats, got_s)
        back = keep.astype(F32) + got.astype(F32)
        if mask == 1:
            back = back.astype(BF)

    keep, send = split_halves(back, bits("x", 1))
    got_s, got = swap_both(stats, send, "x", 2)
    stats = combine(stats, got_s)
    back = lax.ppermute(keep + got.astype(F32), AXES, plane_pairs(True))
    mine_grad = cotangent.astype(F32) + back

    loss, kept = own[:2], own[2:]
    excess = loss - (stats[:2] + jnp.log(stats[2:4]) - stats[4:])
    credit = jnp.where(kept > 0.0, jax.nn.softplus(excess), 0.0)
    weight = credit / (jnp.sum(credit) / jnp.sum(kept))
    both = jnp.stack([excess, weight]).reshape(2, 2, 16, 8, 2).transpose(0, 3, 2, 1, 4).reshape(2, 8, rows)
    excess, weight = both[0], both[1]
    slope = (weight.reshape(8 * rows)[:, None] * u_all.astype(F32)).astype(BF)
    grad_weight = lax.dot_general(
        x_all, slope, (((0,), (0,)), ((), ())), preferred_element_type=F32
    )
    own_weight = lax.dynamic_index_in_dim(weight, co["z"], 0, keepdims=False)
    own_excess = lax.dynamic_index_in_dim(excess, co["z"], 0, keepdims=False)
    grad_input = (own_weight[:, None] * mine_grad).astype(BF)
    return (own_excess, grad_weight, grad_input)


def solution(mesh):
    in_specs = (
        P(("dp", "vocab"), None),
        P(None, ("dp", "vocab")),
        P(("dp", "vocab")),
        P("dp"),
        P("dp", None),
        P("dp", "vocab"),
        P("dp", "vocab"),
        P("dp", "vocab"),
    )
    out_specs = (P("dp"), P("dp", "vocab"), P("dp", "vocab"))
    return jax.shard_map(
        on_device, mesh=mesh, in_specs=in_specs, out_specs=out_specs, check_vma=False
    )
```

```python
import functools

import jax
import jax.numpy as jnp
from jax import lax
from jax.experimental import pallas as pl
from jax.experimental.pallas import tpu as pltpu
from jax.sharding import PartitionSpec as P

AXES = ("dp", "vocab")
NZ, NX, NY, NC = 8, 4, 4, 2
STRIDE = {"z": 32, "x": 8, "y": 2, "c": 1}
SIZE = {"z": NZ, "x": NX, "y": NY, "c": NC}
BF = jnp.bfloat16
F32 = jnp.float32


def coords():
    v = lax.axis_index("vocab")
    return {"z": lax.axis_index("dp"), "x": v // 8, "y": (v // 2) % 4, "c": v % 2}


def ex(a, axis, mask):
    m = STRIDE[axis] * mask
    return lax.ppermute(a, AXES, [(i, i ^ m) for i in range(256)])


def shift(a, axis, k):
    st, n = STRIDE[axis], SIZE[axis]
    pairs = []
    for i in range(256):
        p = (i // st) % n
        pairs.append((i, i + ((p + k) % n - p) * st))
    return lax.ppermute(a, AXES, pairs)


def bit(co, axis, b):
    return ((co[axis] >> b) & 1) == 1


def pair_up(mine, other, hi, dim):
    return jnp.where(hi, jnp.concatenate([other, mine], dim), jnp.concatenate([mine, other], dim))


def gather_direct(a, co, axis, dim):
    me = co[axis]
    blocks = [(0, a)] + [(k, ex(a, axis, k)) for k in (1, 3, 2)]
    buf = jnp.zeros(a.shape[:dim] + (4,) + a.shape[dim:], a.dtype)
    for k, block in blocks:
        buf = place(buf, block, dim, me ^ k)
    return buf


def place(buf, block, dim, pos, col=0):
    start = [jnp.int32(0)] * buf.ndim
    start[dim] = pos % 4
    start[-1] = jnp.int32(col)
    return lax.dynamic_update_slice(buf, jnp.expand_dims(block, dim), tuple(start))


def ring_first(a, axis):
    return shift(a, axis, 1), shift(a, axis, -1)


def ring_second(up, down, axis, cut):
    return shift(up[..., :cut], axis, 1), shift(down[..., cut:], axis, -1)


def ring_stack(a, near, far, co, axis, dim, cut):
    me = co[axis]
    buf = jnp.zeros(a.shape[:dim] + (4,) + a.shape[dim:], a.dtype)
    buf = place(buf, a, dim, me)
    buf = place(buf, near[0], dim, me + 3)
    buf = place(buf, near[1], dim, me + 1)
    buf = place(buf, far[0], dim, me + 2)
    return place(buf, far[1], dim, me + 2, cut)


def halve(a, co, axis, b, dim, dtype):
    hi = bit(co, axis, b)
    first = lax.index_in_dim(a, 0, dim, keepdims=False)
    second = lax.index_in_dim(a, 1, dim, keepdims=False)
    keep = jnp.where(hi, second, first)
    send = jnp.where(hi, first, second).astype(dtype)
    return keep.astype(F32) + ex(send, axis, 1 << b).astype(F32)


def derivative(values):
    sig = jax.nn.sigmoid(values)
    return sig * (1.0 + values * (1.0 - sig))


def plane_pairs(back):
    pairs = [((v // 4) * 32 + 4 * g + v % 4, g * 32 + v) for g in range(8) for v in range(32)]
    return [(j, i) for i, j in pairs] if back else pairs


def logits_kernel(first_ref, p_ref, q_ref, one_ref, two_ref, out_ref, buf, sems):
    half = p_ref.shape[1]
    kb = buf.shape[2]
    steps = buf.shape[0]
    dims = (((1,), (1,)), ((), ()))
    copies = [
        pltpu.make_async_copy(two_ref.at[:, pl.ds(j * kb, kb)], buf.at[j], sems.at[j])
        for j in range(steps)
    ]
    for copy in copies:
        copy.start()

    one = lax.dot_general(
        p_ref[...], one_ref[:, :half], dims, preferred_element_type=F32
    ) + lax.dot_general(q_ref[:, :half], one_ref[:, half:], dims, preferred_element_type=F32)
    for copy in copies:
        copy.wait()
    n = steps // 2
    two = jnp.zeros(one.shape, F32)
    for j in range(steps):
        a_ref = p_ref if j < n else q_ref
        two += lax.dot_general(
            a_ref[:, (j % n) * kb : (j % n + 1) * kb], buf[j], dims, preferred_element_type=F32
        )

    meta = q_ref[:, half:].astype(F32)
    label = (meta[:, 0:1] * 65536.0 + meta[:, 1:2] * 256.0 + meta[:, 2:3]).astype(jnp.int32)
    top = jnp.maximum(jnp.max(one, axis=1, keepdims=True), jnp.max(two, axis=1, keepdims=True))
    total = jnp.sum(jnp.exp(one - top), axis=1, keepdims=True) + jnp.sum(
        jnp.exp(two - top), axis=1, keepdims=True
    )
    ids = lax.broadcasted_iota(jnp.int32, one.shape, 1)
    picked = jnp.sum(
        jnp.where(ids == label - first_ref[0], one, 0.0)
        + jnp.where(ids == label - first_ref[1], two, 0.0),
        axis=1,
        keepdims=True,
    )
    lane = lax.broadcasted_iota(jnp.int32, (one.shape[0], 128), 1)
    cols = jnp.zeros(lane.shape, F32)
    for j, value in enumerate((top, total, picked)):
        cols = jnp.where(lane == j, value, cols)
    out_ref[...] = cols.T[:8]


def local_stats(p, q, head, other_head, first):
    voc, d = head.shape
    rows = p.shape[0]
    steps = 2
    vmem = pl.BlockSpec(memory_space=pltpu.VMEM)
    return pl.pallas_call(
        logits_kernel,
        out_shape=jax.ShapeDtypeStruct((8, rows), F32),
        in_specs=[
            pl.BlockSpec(memory_space=pltpu.SMEM),
            vmem,
            vmem,
            vmem,
            pl.BlockSpec(memory_space=pl.ANY),
        ],
        out_specs=vmem,
        scratch_shapes=[
            pltpu.VMEM((steps, voc, d // steps), BF),
            pltpu.SemaphoreType.DMA((steps,)),
        ],
        compiler_params=pltpu.CompilerParams(vmem_limit_bytes=20 * 1024 * 1024),
        cost_estimate=pl.CostEstimate(
            flops=4 * rows * d * voc,
            bytes_accessed=4 * d * voc + 2 * rows * d,
            transcendentals=2 * rows * voc,
        ),
    )(first, p, q, head, other_head)


def split3(values):
    one = lax.reduce_precision(values, 8, 7)
    two = lax.reduce_precision(values - one, 8, 7)
    return jnp.concatenate([one, two, values - one - two]).astype(BF)


def with_terms(stats, payload):
    terms = split3(stats)
    terms = jnp.pad(terms, ((0, -terms.shape[0] % 16), (0, 0)))
    return jnp.concatenate([payload, terms])


def without_terms(message, n):
    m = message.shape[0] - 3 * n - (-3 * n) % 16
    t = message[m : m + 3 * n].astype(F32)
    return (t[:n] + t[n : 2 * n]) + t[2 * n :], message[:m]


def four_way(stats, parts, co, axis):
    me = co[axis]
    n = stats.shape[0]
    total, own = lax.dynamic_index_in_dim(parts, me, 0, keepdims=False).astype(F32), stats
    for mask in (1, 3, 2):
        part = lax.dynamic_index_in_dim(parts, me ^ mask, 0, keepdims=False)
        got_s, got = without_terms(ex(with_terms(own, part), axis, mask), n)
        total, stats = total + got.astype(F32), combine(stats, got_s)
    return stats, total


def combine(a, b):
    n = a.shape[0] // 3
    top = jnp.maximum(a[:n], b[:n])
    total = a[n : 2 * n] * jnp.exp(a[:n] - top) + b[n : 2 * n] * jnp.exp(b[:n] - top)
    return jnp.concatenate([top, total, a[2 * n :] + b[2 * n :]])


def split_halves(a, hi):
    n = a.shape[0] // 2
    return jnp.where(hi, a[n:], a[:n]), jnp.where(hi, a[:n], a[n:]).astype(BF)


def sync(*values):
    return lax.optimization_barrier(values)


def columns(a, first, size):
    return lax.slice_in_dim(a, first, first + size, axis=a.ndim - 1)


def on_device(
    hidden_ref, head, targets, train_loss, keep_index, layer_input, cotangent, layer_weight
):
    co = coords()
    voc_dev = head.shape[1]
    half = head.shape[0] // 2
    dv = layer_weight.shape[1]
    rows = train_loss.shape[0]
    vocab = lax.axis_index("vocab")
    shard = lax.axis_index("dp") * 32 + vocab

    head = head.T
    other_head = ex(head, "c", 1)

    def bits(axis, b):
        return bit(co, axis, b)

    lane = lax.broadcasted_iota(jnp.int32, (2, 128), 1)
    t = targets[:, None]
    meta = jnp.where(lane == 0, t // 65536, jnp.where(lane == 1, (t // 256) % 256, t % 256))
    meta = jnp.where(lane < 3, meta, 0).astype(BF)
    h = jnp.concatenate([hidden_ref, meta], axis=1)[None]
    h = pair_up(h, ex(h, "z", 4), bits("z", 2), 0)[:, None]
    xs = lax.ppermute(layer_input, AXES, plane_pairs(False))
    h, xs = sync(h, xs)

    h = pair_up(h, ex(h, "z", 2), bits("z", 1), 1)[:, :, None]
    xs = gather_direct(xs, co, "x", 0)
    h, xs = sync(h, xs)

    h = pair_up(h, ex(h, "z", 1), bits("z", 0), 2).reshape(16, 2 * half + 128)
    xs = gather_direct(xs, co, "y", 0).reshape(2, 2, 4, rows, dv)
    xs = jnp.concatenate([xs[:, j].swapaxes(0, 1).reshape(8 * rows, dv) for j in (0, 1)], 1)
    got = ex(xs, "c", 1)
    h, xs, got, other_head = sync(h, xs, got, other_head)

    p = gather_direct(h[:, :half], co, "y", 0)
    q = gather_direct(h[:, half:], co, "x", 0)
    low, high = [
        jnp.concatenate([columns(a, 0, dv), columns(b, 0, dv), columns(a, dv, dv), columns(b, dv, dv)], 1)
        for a, b in ((xs, got), (got, xs))
    ]
    x_all = jnp.where(bits("c", 0), high, low)
    pre = jnp.dot(x_all, layer_weight, preferred_element_type=F32)
    p, q, pre = sync(p, q, pre)

    p_near, q_near = ring_first(p, "x"), ring_first(q, "y")
    pre = halve(pre.reshape(2, 2, 2, rows, dv), co, "z", 0, 2, BF)
    pre = halve(pre, co, "z", 1, 1, BF).astype(BF).reshape(2 * rows, dv)
    p_near, q_near, pre = sync(p_near, q_near, pre)

    p_far, q_far = ring_second(*p_near, "x", half // 2), ring_second(*q_near, "y", half // 2)
    got = ex(jnp.concatenate([pre, cotangent]), "z", 4)
    pre = pre.astype(F32) + got[: 2 * rows].astype(F32)
    cot = pair_up(cotangent, got[2 * rows :], bits("z", 2), 0)
    u = (cot.astype(F32) * derivative(pre)).astype(BF)
    p_far, q_far, u = sync(p_far, q_far, u)

    p = ring_stack(p, p_near, p_far, co, "x", 0, half // 2).reshape(256, half)
    q = ring_stack(q, q_near, q_far, co, "y", 1, half // 2).reshape(256, half + 128)
    first = jnp.stack([shard * voc_dev, (shard ^ 1) * voc_dev]).astype(jnp.int32)
    stats, u = sync(local_stats(p, q, head, other_head, first)[:3], u)

    here = jnp.arange(8, dtype=jnp.int32) == co["z"]
    marks = jnp.any(keep_index[0][None, :] == jnp.arange(rows, dtype=jnp.int32)[:, None], axis=1)
    own = jnp.stack([train_loss, marks.astype(F32)]).reshape(2, 16, 1, 2, 2)
    own = jnp.where(bits("c", 0), own[:, :, :, 1], own[:, :, :, 0])
    own = jnp.where(here[None, None, :, None], own, 0.0).reshape(2, 256)

    got_s = ex(jnp.concatenate([stats, own]), "z", 4)
    u = u.reshape(2, 1, rows, dv)
    full = jnp.zeros((2, 4, rows, dv), BF)
    low_z = co["z"] % 4
    for mask in (0, 1, 3, 2):
        block = ex(u, "z", mask) if mask else u
        full = lax.dynamic_update_slice_in_dim(full, block, low_z ^ mask, 1)
    stats, own = combine(stats, got_s[:3]), own + got_s[3:]
    u_all = full.reshape(8 * rows, dv)
    stats, own, u_all = sync(stats, own, u_all)

    terms = lax.dot_general(
        u_all, layer_weight, (((1,), (1,)), ((), ())), preferred_element_type=F32
    ).astype(BF)
    back = jnp.concatenate([columns(terms, j * dv, dv) for j in (0, 2, 1, 3)])
    hi = bits("c", 0)
    keep, send = split_halves(back, hi)
    got_s, got = without_terms(ex(with_terms(jnp.concatenate([stats, own]), send), "c", 1), 5)
    stats, own = [
        jnp.where(hi, jnp.stack([b, a], 1), jnp.stack([a, b], 1)).reshape(-1, 256)
        for a, b in ((stats, got_s[:3]), (own, got_s[3:]))
    ]
    back = (keep.astype(F32) + got.astype(F32)).astype(BF)
    back = back.reshape(2, 4, 2, rows, dv).transpose(2, 0, 1, 3, 4).reshape(4, 4 * rows, dv)
    stats, back = four_way(stats, back, co, "y")
    stats, back = four_way(stats, back.astype(BF).reshape(4, rows, dv), co, "x")
    back = lax.ppermute(back, AXES, plane_pairs(True))
    mine = jnp.concatenate([stats, own])
    for mask in (1, 3, 2):
        got_s = ex(mine, "z", mask)
        stats, own = combine(stats, got_s[:6]), own + got_s[6:]
    mine_grad = cotangent.astype(F32) + back

    loss, kept = own[:2], own[2:]
    excess = loss - (stats[:2] + jnp.log(stats[2:4]) - stats[4:])
    credit = jnp.where(kept > 0.0, jax.nn.softplus(excess), 0.0)
    weight = credit / (jnp.sum(credit) / jnp.sum(kept))
    both = jnp.stack([excess, weight]).reshape(2, 2, 16, 8, 2).transpose(0, 3, 2, 1, 4).reshape(2, 8, rows)
    excess, weight = both[0], both[1]
    slope = (weight.reshape(8 * rows)[:, None] * u_all.astype(F32)).astype(BF)
    grad_weight = lax.dot_general(
        x_all, slope, (((0,), (0,)), ((), ())), preferred_element_type=F32
    )
    own_weight = lax.dynamic_index_in_dim(weight, co["z"], 0, keepdims=False)
    own_excess = lax.dynamic_index_in_dim(excess, co["z"], 0, keepdims=False)
    grad_input = (own_weight[:, None] * mine_grad).astype(BF)
    return (own_excess, grad_weight, grad_input)


def solution(mesh):
    in_specs = (
        P(("dp", "vocab"), None),
        P(None, ("dp", "vocab")),
        P(("dp", "vocab")),
        P("dp"),
        P("dp", None),
        P("dp", "vocab"),
        P("dp", "vocab"),
        P("dp", "vocab"),
    )
    out_specs = (P("dp"), P("dp", "vocab"), P("dp", "vocab"))
    return jax.shard_map(
        on_device, mesh=mesh, in_specs=in_specs, out_specs=out_specs, check_vma=False
    )
```

```python
import functools

import jax
import jax.numpy as jnp
from jax import lax
from jax.experimental import pallas as pl
from jax.experimental.pallas import tpu as pltpu
from jax.sharding import PartitionSpec as P

AXES = ("dp", "vocab")
NZ, NX, NY, NC = 8, 4, 4, 2
STRIDE = {"z": 32, "x": 8, "y": 2, "c": 1}
SIZE = {"z": NZ, "x": NX, "y": NY, "c": NC}
BF = jnp.bfloat16
F32 = jnp.float32


def coords():
    v = lax.axis_index("vocab")
    return {"z": lax.axis_index("dp"), "x": v // 8, "y": (v // 2) % 4, "c": v % 2}


def ex(a, axis, mask):
    m = STRIDE[axis] * mask
    return lax.ppermute(a, AXES, [(i, i ^ m) for i in range(256)])


def shift(a, axis, k):
    st, n = STRIDE[axis], SIZE[axis]
    pairs = []
    for i in range(256):
        p = (i // st) % n
        pairs.append((i, i + ((p + k) % n - p) * st))
    return lax.ppermute(a, AXES, pairs)


def bit(co, axis, b):
    return ((co[axis] >> b) & 1) == 1


def pair_up(mine, other, hi, dim):
    return jnp.where(hi, jnp.concatenate([other, mine], dim), jnp.concatenate([mine, other], dim))


def gather_direct(a, co, axis, dim):
    me = co[axis]
    blocks = [(0, a)] + [(k, ex(a, axis, k)) for k in (1, 3, 2)]
    buf = jnp.zeros(a.shape[:dim] + (4,) + a.shape[dim:], a.dtype)
    for k, block in blocks:
        buf = place(buf, block, dim, me ^ k)
    return buf


def place(buf, block, dim, pos, col=0):
    start = [jnp.int32(0)] * buf.ndim
    start[dim] = pos % 4
    start[-1] = jnp.int32(col)
    return lax.dynamic_update_slice(buf, jnp.expand_dims(block, dim), tuple(start))


def ring_first(a, axis):
    return shift(a, axis, 1), shift(a, axis, -1)


def ring_second(up, down, axis, cut):
    return shift(up[..., :cut], axis, 1), shift(down[..., cut:], axis, -1)


def ring_stack(a, near, far, co, axis, dim, cut):
    me = co[axis]
    buf = jnp.zeros(a.shape[:dim] + (4,) + a.shape[dim:], a.dtype)
    buf = place(buf, a, dim, me)
    buf = place(buf, near[0], dim, me + 3)
    buf = place(buf, near[1], dim, me + 1)
    buf = place(buf, far[0], dim, me + 2)
    return place(buf, far[1], dim, me + 2, cut)


def halve(a, co, axis, b, dim, dtype):
    hi = bit(co, axis, b)
    first = lax.index_in_dim(a, 0, dim, keepdims=False)
    second = lax.index_in_dim(a, 1, dim, keepdims=False)
    keep = jnp.where(hi, second, first)
    send = jnp.where(hi, first, second).astype(dtype)
    return keep.astype(F32) + ex(send, axis, 1 << b).astype(F32)


def derivative(values):
    sig = jax.nn.sigmoid(values)
    return sig * (1.0 + values * (1.0 - sig))


def plane_pairs(back):
    pairs = [((v // 4) * 32 + 4 * g + v % 4, g * 32 + v) for g in range(8) for v in range(32)]
    return [(j, i) for i, j in pairs] if back else pairs


def logits_kernel(first_ref, p_ref, q_ref, one_ref, two_ref, out_ref, buf, sems):
    half = p_ref.shape[1]
    kb = buf.shape[2]
    steps = buf.shape[0]
    dims = (((1,), (1,)), ((), ()))
    copies = [
        pltpu.make_async_copy(two_ref.at[:, pl.ds(j * kb, kb)], buf.at[j], sems.at[j])
        for j in range(steps)
    ]
    for copy in copies:
        copy.start()

    one = lax.dot_general(
        p_ref[...], one_ref[:, :half], dims, preferred_element_type=F32
    ) + lax.dot_general(q_ref[:, :half], one_ref[:, half:], dims, preferred_element_type=F32)
    n = steps // 2
    two = jnp.zeros(one.shape, F32)
    for j, copy in enumerate(copies):
        copy.wait()
        a_ref = p_ref if j < n else q_ref
        two += lax.dot_general(
            a_ref[:, (j % n) * kb : (j % n + 1) * kb], buf[j], dims, preferred_element_type=F32
        )

    meta = q_ref[:, half:].astype(F32)
    label = (meta[:, 0:1] * 65536.0 + meta[:, 1:2] * 256.0 + meta[:, 2:3]).astype(jnp.int32)
    top = jnp.maximum(jnp.max(one, axis=1, keepdims=True), jnp.max(two, axis=1, keepdims=True))
    total = jnp.sum(jnp.exp(one - top), axis=1, keepdims=True) + jnp.sum(
        jnp.exp(two - top), axis=1, keepdims=True
    )
    ids = lax.broadcasted_iota(jnp.int32, one.shape, 1)
    picked = jnp.sum(
        jnp.where(ids == label - first_ref[0], one, 0.0)
        + jnp.where(ids == label - first_ref[1], two, 0.0),
        axis=1,
        keepdims=True,
    )
    lane = lax.broadcasted_iota(jnp.int32, (one.shape[0], 128), 1)
    cols = jnp.zeros(lane.shape, F32)
    for j, value in enumerate((top, total, picked)):
        cols = jnp.where(lane == j, value, cols)
    out_ref[...] = cols.T[:8]


def local_stats(p, q, head, other_head, first):
    voc, d = head.shape
    rows = p.shape[0]
    steps = 4
    vmem = pl.BlockSpec(memory_space=pltpu.VMEM)
    return pl.pallas_call(
        logits_kernel,
        out_shape=jax.ShapeDtypeStruct((8, rows), F32),
        in_specs=[
            pl.BlockSpec(memory_space=pltpu.SMEM),
            vmem,
            vmem,
            vmem,
            pl.BlockSpec(memory_space=pl.ANY),
        ],
        out_specs=vmem,
        scratch_shapes=[
            pltpu.VMEM((steps, voc, d // steps), BF),
            pltpu.SemaphoreType.DMA((steps,)),
        ],
        compiler_params=pltpu.CompilerParams(vmem_limit_bytes=20 * 1024 * 1024),
        cost_estimate=pl.CostEstimate(
            flops=4 * rows * d * voc,
            bytes_accessed=4 * d * voc + 2 * rows * d,
            transcendentals=2 * rows * voc,
        ),
    )(first, p, q, head, other_head)


def split3(values):
    one = lax.reduce_precision(values, 8, 7)
    two = lax.reduce_precision(values - one, 8, 7)
    return jnp.concatenate([one, two, values - one - two]).astype(BF)


def with_terms(stats, payload):
    terms = split3(stats)
    terms = jnp.pad(terms, ((0, -terms.shape[0] % 16), (0, 0)))
    return jnp.concatenate([payload, terms])


def without_terms(message, n):
    m = message.shape[0] - 3 * n - (-3 * n) % 16
    t = message[m : m + 3 * n].astype(F32)
    return (t[:n] + t[n : 2 * n]) + t[2 * n :], message[:m]


def four_way(stats, parts, co, axis):
    me = co[axis]
    n = stats.shape[0]
    total, own = lax.dynamic_index_in_dim(parts, me, 0, keepdims=False).astype(F32), stats
    for mask in (1, 3, 2):
        part = lax.dynamic_index_in_dim(parts, me ^ mask, 0, keepdims=False)
        got_s, got = without_terms(ex(with_terms(own, part), axis, mask), n)
        total, stats = total + got.astype(F32), combine(stats, got_s)
    return stats, total


def combine(a, b):
    n = a.shape[0] // 3
    top = jnp.maximum(a[:n], b[:n])
    total = a[n : 2 * n] * jnp.exp(a[:n] - top) + b[n : 2 * n] * jnp.exp(b[:n] - top)
    return jnp.concatenate([top, total, a[2 * n :] + b[2 * n :]])


def split_halves(a, hi):
    n = a.shape[0] // 2
    return jnp.where(hi, a[n:], a[:n]), jnp.where(hi, a[:n], a[n:]).astype(BF)


def sync(*values):
    return lax.optimization_barrier(values)


def tail_kernel(z_ref, mine_ref, got_ref, u_ref, x_ref, grad_ref, own_ref):
    mine, got = mine_ref[...], got_ref[...]
    top = jnp.maximum(mine[:2], got[:2])
    total = mine[2:4] * jnp.exp(mine[:2] - top) + got[2:4] * jnp.exp(got[:2] - top)
    rest = mine[4:] + got[4:]
    loss, kept = rest[2:4], rest[4:6]
    excess = loss - (top + jnp.log(total) - rest[0:2])
    credit = jnp.where(kept > 0.0, jax.nn.softplus(excess), 0.0)
    weight = credit / (jnp.sum(credit) / jnp.sum(kept))

    def column(values, n, first):
        r = lax.broadcasted_iota(jnp.int32, (n, 256), 0) + first
        j = lax.broadcasted_iota(jnp.int32, (n, 256), 1)
        at = ((r // 4) % 16) * 16 + (r // 64) * 2 + r % 2
        picked = jnp.where((r // 2) % 2 == 1, values[1:2], values[0:1])
        return jnp.sum(jnp.where(at == j, picked, 0.0), axis=1, keepdims=True)

    slope = (column(weight, 512, 0) * u_ref[...].astype(F32)).astype(BF)
    grad_ref[...] = lax.dot_general(
        x_ref[...], slope, (((0,), (0,)), ((), ())), preferred_element_type=F32
    )
    first = z_ref[0] * 64
    lane = lax.broadcasted_iota(jnp.int32, (64, 128), 1)
    own_ref[...] = jnp.where(lane == 0, column(weight, 64, first), column(excess, 64, first))


def tail(z, mine, got, u_all, x_all):
    vmem = pl.BlockSpec(memory_space=pltpu.VMEM)
    out = (
        jax.ShapeDtypeStruct((x_all.shape[1], u_all.shape[1]), F32),
        jax.ShapeDtypeStruct((64, 128), F32),
    )
    return pl.pallas_call(
        tail_kernel,
        out_shape=out,
        in_specs=[pl.BlockSpec(memory_space=pltpu.SMEM)] + [vmem] * 4,
        out_specs=(vmem, vmem),
        compiler_params=pltpu.CompilerParams(vmem_limit_bytes=16 * 1024 * 1024),
        cost_estimate=pl.CostEstimate(
            flops=2 * x_all.size * u_all.shape[1], bytes_accessed=4 * x_all.size, transcendentals=4096
        ),
    )(z, mine, got, u_all, x_all)


def columns(a, first, size):
    return lax.slice_in_dim(a, first, first + size, axis=a.ndim - 1)


def on_device(
    hidden_ref, head, targets, train_loss, keep_index, layer_input, cotangent, layer_weight
):
    co = coords()
    voc_dev = head.shape[1]
    half = head.shape[0] // 2
    dv = layer_weight.shape[1]
    rows = train_loss.shape[0]
    vocab = lax.axis_index("vocab")
    shard = lax.axis_index("dp") * 32 + vocab

    head = head.T
    other_head = ex(head, "c", 1)

    def bits(axis, b):
        return bit(co, axis, b)

    lane = lax.broadcasted_iota(jnp.int32, (2, 128), 1)
    t = targets[:, None]
    meta = jnp.where(lane == 0, t // 65536, jnp.where(lane == 1, (t // 256) % 256, t % 256))
    meta = jnp.where(lane < 3, meta, 0).astype(BF)
    h = jnp.concatenate([hidden_ref, meta], axis=1)[None]
    h = pair_up(h, ex(h, "z", 4), bits("z", 2), 0)[:, None]
    xs = lax.ppermute(layer_input, AXES, plane_pairs(False))

    h = pair_up(h, ex(h, "z", 2), bits("z", 1), 1)[:, :, None]
    xs = gather_direct(xs, co, "x", 0)
    h, xs = sync(h, xs)

    h = pair_up(h, ex(h, "z", 1), bits("z", 0), 2).reshape(16, 2 * half + 128)
    xs = gather_direct(xs, co, "y", 0).reshape(2, 2, 4, rows, dv)
    xs = jnp.concatenate([xs[:, j].swapaxes(0, 1).reshape(8 * rows, dv) for j in (0, 1)], 1)
    h, xs, other_head = sync(h, xs, other_head)

    p, q = h[:, :half], h[:, half:]
    p = gather_direct(p, co, "y", 0)
    got = ex(xs, "c", 1)
    p, q, xs, got = sync(p, q, xs, got)

    q = gather_direct(q, co, "x", 0)
    low, high = [
        jnp.concatenate([columns(a, 0, dv), columns(b, 0, dv), columns(a, dv, dv), columns(b, dv, dv)], 1)
        for a, b in ((xs, got), (got, xs))
    ]
    x_all = jnp.where(bits("c", 0), high, low)
    pre = jnp.dot(x_all, layer_weight, preferred_element_type=F32)
    p, q, pre = sync(p, q, pre)

    p_near, q_near = ring_first(p, "x"), ring_first(q, "y")
    pre = halve(pre.reshape(2, 2, 2, rows, dv), co, "z", 0, 2, BF)
    pre = halve(pre, co, "z", 1, 1, BF).astype(BF).reshape(2 * rows, dv)
    p_near, q_near, pre = sync(p_near, q_near, pre)

    p_far, q_far = ring_second(*p_near, "x", half // 2), ring_second(*q_near, "y", half // 2)
    got = ex(jnp.concatenate([pre, cotangent]), "z", 4)
    pre = pre.astype(F32) + got[: 2 * rows].astype(F32)
    cot = pair_up(cotangent, got[2 * rows :], bits("z", 2), 0)
    u = (cot.astype(F32) * derivative(pre)).astype(BF)
    p_far, q_far, u = sync(p_far, q_far, u)

    p = ring_stack(p, p_near, p_far, co, "x", 0, half // 2).reshape(256, half)
    q = ring_stack(q, q_near, q_far, co, "y", 1, half // 2).reshape(256, half + 128)
    first = jnp.stack([shard * voc_dev, (shard ^ 1) * voc_dev]).astype(jnp.int32)
    stats, u = sync(local_stats(p, q, head, other_head, first)[:3], u)

    here = jnp.arange(8, dtype=jnp.int32) == co["z"]
    marks = jnp.any(keep_index[0][None, :] == jnp.arange(rows, dtype=jnp.int32)[:, None], axis=1)
    own = jnp.stack([train_loss, marks.astype(F32)]).reshape(2, 16, 1, 2, 2)
    own = jnp.where(bits("c", 0), own[:, :, :, 1], own[:, :, :, 0])
    own = jnp.where(here[None, None, :, None], own, 0.0).reshape(2, 256)

    u_all = jnp.zeros((2, 4, rows, dv), BF)
    u_all = lax.dynamic_update_slice_in_dim(u_all, u.reshape(2, 1, rows, dv), co["z"] % 4, 1)
    mine = jnp.concatenate([stats, own])
    for mask in (1, 3, 2):
        got_s, got = without_terms(ex(with_terms(mine, u), "z", mask), 5)
        stats, own = combine(stats, got_s[:3]), own + got_s[3:]
        got = got.reshape(2, 1, rows, dv)
        u_all = lax.dynamic_update_slice_in_dim(u_all, got, (co["z"] % 4) ^ mask, 1)
    u_all = u_all.reshape(8 * rows, dv)
    stats, own, u_all = sync(stats, own, u_all)

    terms = lax.dot_general(
        u_all, layer_weight, (((1,), (1,)), ((), ())), preferred_element_type=F32
    ).astype(BF)
    back = jnp.concatenate([columns(terms, j * dv, dv) for j in (0, 2, 1, 3)])
    hi = bits("c", 0)
    keep, send = split_halves(back, hi)
    got_s, got = without_terms(ex(with_terms(jnp.concatenate([stats, own]), send), "c", 1), 5)
    stats, own = [
        jnp.where(hi, jnp.stack([b, a], 1), jnp.stack([a, b], 1)).reshape(-1, 256)
        for a, b in ((stats, got_s[:3]), (own, got_s[3:]))
    ]
    back = (keep.astype(F32) + got.astype(F32)).astype(BF)
    back = back.reshape(2, 4, 2, rows, dv).transpose(2, 0, 1, 3, 4).reshape(4, 4 * rows, dv)
    stats, back = four_way(stats, back, co, "y")
    stats, back = four_way(stats, back.astype(BF).reshape(4, rows, dv), co, "x")
    back = lax.ppermute(back.astype(BF), AXES, plane_pairs(True))
    mine = jnp.concatenate([stats, own])
    got_s = ex(mine, "z", 4)
    mine_grad = cotangent.astype(F32) + back.astype(F32)
    grad_weight, own = tail(co["z"].astype(jnp.int32)[None], mine, got_s, u_all, x_all)
    grad_input = (own[:, :1] * mine_grad).astype(BF)
    return (own[:, 1], grad_weight, grad_input)


def solution(mesh):
    in_specs = (
        P(("dp", "vocab"), None),
        P(None, ("dp", "vocab")),
        P(("dp", "vocab")),
        P("dp"),
        P("dp", None),
        P("dp", "vocab"),
        P("dp", "vocab"),
        P("dp", "vocab"),
    )
    out_specs = (P("dp"), P("dp", "vocab"), P("dp", "vocab"))
    return jax.shard_map(
        on_device, mesh=mesh, in_specs=in_specs, out_specs=out_specs, check_vma=False
    )
```

```python
import functools

import jax
import jax.numpy as jnp
from jax import lax
from jax.experimental import pallas as pl
from jax.experimental.pallas import tpu as pltpu
from jax.sharding import PartitionSpec as P

AXES = ("dp", "vocab")
NZ, NX, NY, NC = 8, 4, 4, 2
STRIDE = {"z": 32, "x": 8, "y": 2, "c": 1}
SIZE = {"z": NZ, "x": NX, "y": NY, "c": NC}
BF = jnp.bfloat16
F32 = jnp.float32


def coords():
    v = lax.axis_index("vocab")
    return {"z": lax.axis_index("dp"), "x": v // 8, "y": (v // 2) % 4, "c": v % 2}


def ex(a, axis, mask):
    m = STRIDE[axis] * mask
    return lax.ppermute(a, AXES, [(i, i ^ m) for i in range(256)])


def shift(a, axis, k):
    st, n = STRIDE[axis], SIZE[axis]
    pairs = []
    for i in range(256):
        p = (i // st) % n
        pairs.append((i, i + ((p + k) % n - p) * st))
    return lax.ppermute(a, AXES, pairs)


def bit(co, axis, b):
    return ((co[axis] >> b) & 1) == 1


def pair_up(mine, other, hi, dim):
    return jnp.where(hi, jnp.concatenate([other, mine], dim), jnp.concatenate([mine, other], dim))


def gather_direct(a, co, axis, dim):
    me = co[axis]
    blocks = [(0, a)] + [(k, ex(a, axis, k)) for k in (1, 3, 2)]
    buf = jnp.zeros(a.shape[:dim] + (4,) + a.shape[dim:], a.dtype)
    for k, block in blocks:
        buf = place(buf, block, dim, me ^ k)
    return buf


def place(buf, block, dim, pos, col=0):
    start = [jnp.int32(0)] * buf.ndim
    start[dim] = pos % 4
    start[-1] = jnp.int32(col)
    return lax.dynamic_update_slice(buf, jnp.expand_dims(block, dim), tuple(start))


def ring_first(a, axis):
    return shift(a, axis, 1), shift(a, axis, -1)


def ring_second(up, down, axis, cut):
    return shift(up[..., :cut], axis, 1), shift(down[..., cut:], axis, -1)


def ring_stack(a, near, far, co, axis, dim, cut):
    me = co[axis]
    buf = jnp.zeros(a.shape[:dim] + (4,) + a.shape[dim:], a.dtype)
    buf = place(buf, a, dim, me)
    buf = place(buf, near[0], dim, me + 3)
    buf = place(buf, near[1], dim, me + 1)
    buf = place(buf, far[0], dim, me + 2)
    return place(buf, far[1], dim, me + 2, cut)


def halve(a, co, axis, b, dim, dtype):
    hi = bit(co, axis, b)
    first = lax.index_in_dim(a, 0, dim, keepdims=False)
    second = lax.index_in_dim(a, 1, dim, keepdims=False)
    keep = jnp.where(hi, second, first)
    send = jnp.where(hi, first, second).astype(dtype)
    return keep.astype(F32) + ex(send, axis, 1 << b).astype(F32)


def derivative(values):
    sig = jax.nn.sigmoid(values)
    return sig * (1.0 + values * (1.0 - sig))


def plane_pairs(back):
    pairs = [((v // 4) * 32 + 4 * g + v % 4, g * 32 + v) for g in range(8) for v in range(32)]
    return [(j, i) for i, j in pairs] if back else pairs


def logits_kernel(first_ref, p_ref, q_ref, one_ref, two_ref, out_ref, buf, sems):
    half = p_ref.shape[1]
    kb = buf.shape[2]
    steps = buf.shape[0]
    dims = (((1,), (1,)), ((), ()))
    copies = [
        pltpu.make_async_copy(two_ref.at[:, pl.ds(j * kb, kb)], buf.at[j], sems.at[j])
        for j in range(steps)
    ]
    for copy in copies:
        copy.start()

    one = lax.dot_general(
        p_ref[...], one_ref[:, :half], dims, preferred_element_type=F32
    ) + lax.dot_general(q_ref[:, :half], one_ref[:, half:], dims, preferred_element_type=F32)
    n = steps // 2
    two = jnp.zeros(one.shape, F32)
    for j, copy in enumerate(copies):
        copy.wait()
        a_ref = p_ref if j < n else q_ref
        two += lax.dot_general(
            a_ref[:, (j % n) * kb : (j % n + 1) * kb], buf[j], dims, preferred_element_type=F32
        )

    meta = q_ref[:, half:].astype(F32)
    label = (meta[:, 0:1] * 65536.0 + meta[:, 1:2] * 256.0 + meta[:, 2:3]).astype(jnp.int32)
    top = jnp.maximum(jnp.max(one, axis=1, keepdims=True), jnp.max(two, axis=1, keepdims=True))
    total = jnp.sum(jnp.exp(one - top), axis=1, keepdims=True) + jnp.sum(
        jnp.exp(two - top), axis=1, keepdims=True
    )
    ids = lax.broadcasted_iota(jnp.int32, one.shape, 1)
    picked = jnp.sum(
        jnp.where(ids == label - first_ref[0], one, 0.0)
        + jnp.where(ids == label - first_ref[1], two, 0.0),
        axis=1,
        keepdims=True,
    )
    lane = lax.broadcasted_iota(jnp.int32, (one.shape[0], 128), 1)
    cols = jnp.zeros(lane.shape, F32)
    for j, value in enumerate((top, total, picked)):
        cols = jnp.where(lane == j, value, cols)
    out_ref[...] = cols.T[:8]


def local_stats(p, q, head, other_head, first):
    voc, d = head.shape
    rows = p.shape[0]
    steps = 4
    vmem = pl.BlockSpec(memory_space=pltpu.VMEM)
    return pl.pallas_call(
        logits_kernel,
        out_shape=jax.ShapeDtypeStruct((8, rows), F32),
        in_specs=[
            pl.BlockSpec(memory_space=pltpu.SMEM),
            vmem,
            vmem,
            vmem,
            pl.BlockSpec(memory_space=pl.ANY),
        ],
        out_specs=vmem,
        scratch_shapes=[
            pltpu.VMEM((steps, voc, d // steps), BF),
            pltpu.SemaphoreType.DMA((steps,)),
        ],
        compiler_params=pltpu.CompilerParams(vmem_limit_bytes=20 * 1024 * 1024),
        cost_estimate=pl.CostEstimate(
            flops=4 * rows * d * voc,
            bytes_accessed=4 * d * voc + 2 * rows * d,
            transcendentals=2 * rows * voc,
        ),
    )(first, p, q, head, other_head)


def split3(values):
    one = lax.reduce_precision(values, 8, 7)
    two = lax.reduce_precision(values - one, 8, 7)
    return jnp.concatenate([one, two, values - one - two]).astype(BF)


def with_terms(stats, payload):
    terms = split3(stats)
    terms = jnp.pad(terms, ((0, -terms.shape[0] % 16), (0, 0)))
    return jnp.concatenate([payload, terms])


def without_terms(message, n):
    m = message.shape[0] - 3 * n - (-3 * n) % 16
    t = message[m : m + 3 * n].astype(F32)
    return (t[:n] + t[n : 2 * n]) + t[2 * n :], message[:m]


def four_way(stats, parts, co, axis):
    me = co[axis]
    n = stats.shape[0]
    total, own = lax.dynamic_index_in_dim(parts, me, 0, keepdims=False).astype(F32), stats
    for mask in (1, 3, 2):
        part = lax.dynamic_index_in_dim(parts, me ^ mask, 0, keepdims=False)
        got_s, got = without_terms(ex(with_terms(own, part), axis, mask), n)
        total, stats = total + got.astype(F32), combine(stats, got_s)
    return stats, total


def combine(a, b):
    n = a.shape[0] // 3
    top = jnp.maximum(a[:n], b[:n])
    total = a[n : 2 * n] * jnp.exp(a[:n] - top) + b[n : 2 * n] * jnp.exp(b[:n] - top)
    return jnp.concatenate([top, total, a[2 * n :] + b[2 * n :]])


def split_halves(a, hi):
    n = a.shape[0] // 2
    return jnp.where(hi, a[n:], a[:n]), jnp.where(hi, a[:n], a[n:]).astype(BF)


def sync(*values):
    return lax.optimization_barrier(values)


def tail_kernel(z_ref, mine_ref, got_ref, u_ref, x_ref, grad_ref, own_ref):
    mine, got = mine_ref[...], got_ref[...]
    top = jnp.maximum(mine[:2], got[:2])
    total = mine[2:4] * jnp.exp(mine[:2] - top) + got[2:4] * jnp.exp(got[:2] - top)
    rest = mine[4:] + got[4:]
    loss, kept = rest[2:4], rest[4:6]
    excess = loss - (top + jnp.log(total) - rest[0:2])
    credit = jnp.where(kept > 0.0, jax.nn.softplus(excess), 0.0)
    weight = credit / (jnp.sum(credit) / jnp.sum(jnp.where(kept > 0.0, 1.0, 0.0)))

    def by_slot(values):
        n = u_ref.shape[0]
        slots = n // 8
        r = lax.broadcasted_iota(jnp.int32, (n, 256), 0)
        j = lax.broadcasted_iota(jnp.int32, (n, 256), 1)
        code = r + 1
        for g in range(1, 8):
            code = code + jnp.where(r >= g * slots, 64 - slots, 0)
        at = ((j // 2) % 8) * 64
        number = kept.astype(jnp.int32)
        hits = [jnp.where(at + number[c : c + 1] == code, values[c : c + 1], 0.0) for c in (0, 1)]
        return jnp.sum(hits[0] + hits[1], axis=1, keepdims=True)

    def column(values, n, first):
        r = lax.broadcasted_iota(jnp.int32, (n, 256), 0) + first
        j = lax.broadcasted_iota(jnp.int32, (n, 256), 1)
        at = ((r // 4) % 16) * 16 + (r // 64) * 2 + r % 2
        picked = jnp.where((r // 2) % 2 == 1, values[1:2], values[0:1])
        return jnp.sum(jnp.where(at == j, picked, 0.0), axis=1, keepdims=True)

    slope = (by_slot(weight) * u_ref[...].astype(F32)).astype(BF)
    grad_ref[...] = lax.dot_general(
        x_ref[...], slope, (((0,), (0,)), ((), ())), preferred_element_type=F32
    )
    first = z_ref[0] * 64
    lane = lax.broadcasted_iota(jnp.int32, (64, 128), 1)
    own_ref[...] = jnp.where(lane == 0, column(weight, 64, first), column(excess, 64, first))


def tail(z, mine, got, u_all, x_all):
    vmem = pl.BlockSpec(memory_space=pltpu.VMEM)
    out = (
        jax.ShapeDtypeStruct((x_all.shape[1], u_all.shape[1]), F32),
        jax.ShapeDtypeStruct((64, 128), F32),
    )
    return pl.pallas_call(
        tail_kernel,
        out_shape=out,
        in_specs=[pl.BlockSpec(memory_space=pltpu.SMEM)] + [vmem] * 4,
        out_specs=(vmem, vmem),
        compiler_params=pltpu.CompilerParams(vmem_limit_bytes=16 * 1024 * 1024),
        cost_estimate=pl.CostEstimate(
            flops=2 * x_all.size * u_all.shape[1], bytes_accessed=4 * x_all.size, transcendentals=4096
        ),
    )(z, mine, got, u_all, x_all)


def columns(a, first, size):
    return lax.slice_in_dim(a, first, first + size, axis=a.ndim - 1)


def on_device(
    hidden_ref, head, targets, train_loss, keep_index, layer_input, cotangent, layer_weight
):
    co = coords()
    voc_dev = head.shape[1]
    half = head.shape[0] // 2
    dv = layer_weight.shape[1]
    rows = train_loss.shape[0]
    slots = keep_index.shape[1]
    vocab = lax.axis_index("vocab")
    shard = lax.axis_index("dp") * 32 + vocab

    head = head.T
    other_head = ex(head, "c", 1)

    def bits(axis, b):
        return bit(co, axis, b)

    lane = lax.broadcasted_iota(jnp.int32, (2, 128), 1)
    t = targets[:, None]
    meta = jnp.where(lane == 0, t // 65536, jnp.where(lane == 1, (t // 256) % 256, t % 256))
    meta = jnp.where(lane < 3, meta, 0).astype(BF)
    h = jnp.concatenate([hidden_ref, meta], axis=1)[None]
    h = pair_up(h, ex(h, "z", 4), bits("z", 2), 0)[:, None]
    hot = (keep_index[0][:, None] == jnp.arange(rows, dtype=jnp.int32)[None, :]).astype(BF)
    inputs, cotangent_kept = [
        jnp.dot(hot, full, preferred_element_type=F32).astype(BF) for full in (layer_input, cotangent)
    ]
    xs = lax.ppermute(inputs, AXES, plane_pairs(False))

    h = pair_up(h, ex(h, "z", 2), bits("z", 1), 1)[:, :, None]
    xs = gather_direct(xs, co, "x", 0)
    h, xs = sync(h, xs)

    h = pair_up(h, ex(h, "z", 1), bits("z", 0), 2).reshape(16, 2 * half + 128)
    xs = gather_direct(xs, co, "y", 0).reshape(2, 2, 4, slots, dv)
    xs = jnp.concatenate([xs[:, j].swapaxes(0, 1).reshape(8 * slots, dv) for j in (0, 1)], 1)
    h, xs, other_head = sync(h, xs, other_head)

    p, q = h[:, :half], h[:, half:]
    p = gather_direct(p, co, "y", 0)
    got = ex(xs, "c", 1)
    p, q, xs, got = sync(p, q, xs, got)

    q = gather_direct(q, co, "x", 0)
    low, high = [
        jnp.concatenate([columns(a, 0, dv), columns(b, 0, dv), columns(a, dv, dv), columns(b, dv, dv)], 1)
        for a, b in ((xs, got), (got, xs))
    ]
    x_all = jnp.where(bits("c", 0), high, low)
    pre = jnp.dot(x_all, layer_weight, preferred_element_type=F32)
    p, q, pre = sync(p, q, pre)

    p_near, q_near = ring_first(p, "x"), ring_first(q, "y")
    pre = halve(pre.reshape(2, 2, 2, slots, dv), co, "z", 0, 2, BF)
    pre = halve(pre, co, "z", 1, 1, BF).astype(BF).reshape(2 * slots, dv)
    p_near, q_near, pre = sync(p_near, q_near, pre)

    p_far, q_far = ring_second(*p_near, "x", half // 2), ring_second(*q_near, "y", half // 2)
    got = ex(jnp.concatenate([pre, cotangent_kept]), "z", 4)
    pre = pre.astype(F32) + got[: 2 * slots].astype(F32)
    cot = pair_up(cotangent_kept, got[2 * slots :], bits("z", 2), 0)
    u = (cot.astype(F32) * derivative(pre)).astype(BF)
    p_far, q_far, u = sync(p_far, q_far, u)

    p = ring_stack(p, p_near, p_far, co, "x", 0, half // 2).reshape(256, half)
    q = ring_stack(q, q_near, q_far, co, "y", 1, half // 2).reshape(256, half + 128)
    first = jnp.stack([shard * voc_dev, (shard ^ 1) * voc_dev]).astype(jnp.int32)
    stats, u = sync(local_stats(p, q, head, other_head, first)[:3], u)

    here = jnp.arange(8, dtype=jnp.int32) == co["z"]
    number = jnp.arange(1, slots + 1, dtype=jnp.int32)
    here_kept = keep_index[0][None, :] == jnp.arange(rows, dtype=jnp.int32)[:, None]
    marks = jnp.sum(jnp.where(here_kept, number[None, :], 0), axis=1)
    own = jnp.stack([train_loss, marks.astype(F32)]).reshape(2, 16, 1, 2, 2)
    own = jnp.where(bits("c", 0), own[:, :, :, 1], own[:, :, :, 0])
    own = jnp.where(here[None, None, :, None], own, 0.0).reshape(2, 256)

    u_all = jnp.zeros((2, 4, slots, dv), BF)
    u_all = lax.dynamic_update_slice_in_dim(u_all, u.reshape(2, 1, slots, dv), co["z"] % 4, 1)
    mine = jnp.concatenate([stats, own])
    for mask in (1, 3, 2):
        got_s, got = without_terms(ex(with_terms(mine, u), "z", mask), 5)
        stats, own = combine(stats, got_s[:3]), own + got_s[3:]
        got = got.reshape(2, 1, slots, dv)
        u_all = lax.dynamic_update_slice_in_dim(u_all, got, (co["z"] % 4) ^ mask, 1)
    u_all = u_all.reshape(8 * slots, dv)
    stats, own, u_all = sync(stats, own, u_all)

    terms = lax.dot_general(
        u_all, layer_weight, (((1,), (1,)), ((), ())), preferred_element_type=F32
    ).astype(BF)
    back = jnp.concatenate([columns(terms, j * dv, dv) for j in (0, 2, 1, 3)])
    hi = bits("c", 0)
    keep, send = split_halves(back, hi)
    got_s, got = without_terms(ex(with_terms(jnp.concatenate([stats, own]), send), "c", 1), 5)
    stats, own = [
        jnp.where(hi, jnp.stack([b, a], 1), jnp.stack([a, b], 1)).reshape(-1, 256)
        for a, b in ((stats, got_s[:3]), (own, got_s[3:]))
    ]
    back = (keep.astype(F32) + got.astype(F32)).astype(BF)
    back = back.reshape(2, 4, 2, slots, dv).transpose(2, 0, 1, 3, 4).reshape(4, 4 * slots, dv)
    stats, back = four_way(stats, back, co, "y")
    stats, back = four_way(stats, back.astype(BF).reshape(4, slots, dv), co, "x")
    back = lax.ppermute(back.astype(BF), AXES, plane_pairs(True))
    mine = jnp.concatenate([stats, own])
    got_s = ex(mine, "z", 4)
    spread = lax.dot_general(hot, back, (((0,), (0,)), ((), ())), preferred_element_type=F32)
    mine_grad = cotangent.astype(F32) + spread
    grad_weight, own = tail(co["z"].astype(jnp.int32)[None], mine, got_s, u_all, x_all)
    grad_input = (own[:, :1] * mine_grad).astype(BF)
    return (own[:, 1], grad_weight, grad_input)


def solution(mesh):
    in_specs = (
        P(("dp", "vocab"), None),
        P(None, ("dp", "vocab")),
        P(("dp", "vocab")),
        P("dp"),
        P("dp", None),
        P("dp", "vocab"),
        P("dp", "vocab"),
        P("dp", "vocab"),
    )
    out_specs = (P("dp"), P("dp", "vocab"), P("dp", "vocab"))
    return jax.shard_map(
        on_device, mesh=mesh, in_specs=in_specs, out_specs=out_specs, check_vma=False
    )
```

```python
import functools

import jax
import jax.numpy as jnp
from jax import lax
from jax.experimental import pallas as pl
from jax.experimental.pallas import tpu as pltpu
from jax.sharding import PartitionSpec as P

AXES = ("dp", "vocab")
NZ, NX, NY, NC = 8, 4, 4, 2
STRIDE = {"z": 32, "x": 8, "y": 2, "c": 1}
SIZE = {"z": NZ, "x": NX, "y": NY, "c": NC}
BF = jnp.bfloat16
F32 = jnp.float32


def coords():
    v = lax.axis_index("vocab")
    return {"z": lax.axis_index("dp"), "x": v // 8, "y": (v // 2) % 4, "c": v % 2}


def ex(a, axis, mask):
    m = STRIDE[axis] * mask
    return lax.ppermute(a, AXES, [(i, i ^ m) for i in range(256)])


def shift(a, axis, k):
    st, n = STRIDE[axis], SIZE[axis]
    pairs = []
    for i in range(256):
        p = (i // st) % n
        pairs.append((i, i + ((p + k) % n - p) * st))
    return lax.ppermute(a, AXES, pairs)


def bit(co, axis, b):
    return ((co[axis] >> b) & 1) == 1


def pair_up(mine, other, hi, dim):
    return jnp.where(hi, jnp.concatenate([other, mine], dim), jnp.concatenate([mine, other], dim))


def gather_direct(a, co, axis, dim):
    me = co[axis]
    blocks = [(0, a)] + [(k, ex(a, axis, k)) for k in (1, 3, 2)]
    buf = jnp.zeros(a.shape[:dim] + (4,) + a.shape[dim:], a.dtype)
    for k, block in blocks:
        buf = place(buf, block, dim, me ^ k)
    return buf


def place(buf, block, dim, pos, col=0):
    start = [jnp.int32(0)] * buf.ndim
    start[dim] = pos % 4
    start[-1] = jnp.int32(col)
    return lax.dynamic_update_slice(buf, jnp.expand_dims(block, dim), tuple(start))


def ring_first(a, axis):
    return shift(a, axis, 1), shift(a, axis, -1)


def ring_second(up, down, axis, cut):
    return shift(up[..., :cut], axis, 1), shift(down[..., cut:], axis, -1)


def ring_stack(a, near, far, co, axis, dim, cut):
    me = co[axis]
    buf = jnp.zeros(a.shape[:dim] + (4,) + a.shape[dim:], a.dtype)
    buf = place(buf, a, dim, me)
    buf = place(buf, near[0], dim, me + 3)
    buf = place(buf, near[1], dim, me + 1)
    buf = place(buf, far[0], dim, me + 2)
    return place(buf, far[1], dim, me + 2, cut)


def halve(a, co, axis, b, dim, dtype):
    hi = bit(co, axis, b)
    first = lax.index_in_dim(a, 0, dim, keepdims=False)
    second = lax.index_in_dim(a, 1, dim, keepdims=False)
    keep = jnp.where(hi, second, first)
    send = jnp.where(hi, first, second).astype(dtype)
    return keep.astype(F32) + ex(send, axis, 1 << b).astype(F32)


def derivative(values):
    sig = jax.nn.sigmoid(values)
    return sig * (1.0 + values * (1.0 - sig))


def plane_pairs(back):
    pairs = [((v // 4) * 32 + 4 * g + v % 4, g * 32 + v) for g in range(8) for v in range(32)]
    return [(j, i) for i, j in pairs] if back else pairs


def logits_kernel(first_ref, p_ref, q_ref, one_ref, two_ref, out_ref):
    half = p_ref.shape[1]
    dims = (((1,), (1,)), ((), ()))

    def logits(w_ref):
        return lax.dot_general(
            p_ref[...], w_ref[:, :half], dims, preferred_element_type=F32
        ) + lax.dot_general(
            q_ref[:, :half], w_ref[:, half:], dims, preferred_element_type=F32
        )

    meta = q_ref[:, half:].astype(F32)
    label = (meta[:, 0:1] * 65536.0 + meta[:, 1:2] * 256.0 + meta[:, 2:3]).astype(jnp.int32)
    two, one = logits(two_ref), logits(one_ref)
    top = jnp.maximum(jnp.max(one, axis=1, keepdims=True), jnp.max(two, axis=1, keepdims=True))
    total = jnp.sum(jnp.exp(one - top), axis=1, keepdims=True) + jnp.sum(
        jnp.exp(two - top), axis=1, keepdims=True
    )
    ids = lax.broadcasted_iota(jnp.int32, one.shape, 1)
    picked = jnp.sum(
        jnp.where(ids == label - first_ref[0], one, 0.0)
        + jnp.where(ids == label - first_ref[1], two, 0.0),
        axis=1,
        keepdims=True,
    )
    lane = lax.broadcasted_iota(jnp.int32, (one.shape[0], 128), 1)
    cols = jnp.zeros(lane.shape, F32)
    for j, value in enumerate((top, total, picked)):
        cols = jnp.where(lane == j, value, cols)
    out_ref[...] = cols.T[:8]


def local_stats(p, q, head, other_head, first):
    voc, d = head.shape
    rows = p.shape[0]
    return pl.pallas_call(
        logits_kernel,
        out_shape=jax.ShapeDtypeStruct((8, rows), F32),
        in_specs=[pl.BlockSpec(memory_space=pltpu.SMEM)]
        + [pl.BlockSpec(memory_space=pltpu.VMEM)] * 4,
        out_specs=pl.BlockSpec(memory_space=pltpu.VMEM),
        compiler_params=pltpu.CompilerParams(vmem_limit_bytes=20 * 1024 * 1024),
        cost_estimate=pl.CostEstimate(
            flops=4 * rows * d * voc,
            bytes_accessed=4 * d * voc + 2 * rows * d,
            transcendentals=2 * rows * voc,
        ),
    )(first, p, q, head, other_head)


def split3(values):
    one = lax.reduce_precision(values, 8, 7)
    two = lax.reduce_precision(values - one, 8, 7)
    return jnp.concatenate([one, two, values - one - two]).astype(BF)


def with_terms(stats, payload):
    terms = split3(stats)
    terms = jnp.pad(terms, ((0, -terms.shape[0] % 16), (0, 0)))
    return jnp.concatenate([payload, terms])


def without_terms(message, n):
    m = message.shape[0] - 3 * n - (-3 * n) % 16
    t = message[m : m + 3 * n].astype(F32)
    return (t[:n] + t[n : 2 * n]) + t[2 * n :], message[:m]


def four_way(stats, parts, co, axis):
    me = co[axis]
    n = stats.shape[0]
    total, own = lax.dynamic_index_in_dim(parts, me, 0, keepdims=False).astype(F32), stats
    for mask in (1, 3, 2):
        part = lax.dynamic_index_in_dim(parts, me ^ mask, 0, keepdims=False)
        got_s, got = without_terms(ex(with_terms(own, part), axis, mask), n)
        total, stats = total + got.astype(F32), combine(stats, got_s)
    return stats, total


def combine(a, b):
    n = a.shape[0] // 3
    top = jnp.maximum(a[:n], b[:n])
    total = a[n : 2 * n] * jnp.exp(a[:n] - top) + b[n : 2 * n] * jnp.exp(b[:n] - top)
    return jnp.concatenate([top, total, a[2 * n :] + b[2 * n :]])


def split_halves(a, hi):
    n = a.shape[0] // 2
    return jnp.where(hi, a[n:], a[:n]), jnp.where(hi, a[:n], a[n:]).astype(BF)


def sync(*values):
    return lax.optimization_barrier(values)


def tail_kernel(z_ref, mine_ref, got_ref, u_ref, x_ref, grad_ref, own_ref):
    mine, got = mine_ref[...], got_ref[...]
    top = jnp.maximum(mine[:2], got[:2])
    total = mine[2:4] * jnp.exp(mine[:2] - top) + got[2:4] * jnp.exp(got[:2] - top)
    rest = mine[4:] + got[4:]
    loss, kept = rest[2:4], rest[4:6]
    excess = loss - (top + jnp.log(total) - rest[0:2])
    credit = jnp.where(kept > 0.0, jax.nn.softplus(excess), 0.0)
    weight = credit / (jnp.sum(credit) / jnp.sum(jnp.where(kept > 0.0, 1.0, 0.0)))

    def by_slot(values):
        n = u_ref.shape[0]
        slots = n // 8
        r = lax.broadcasted_iota(jnp.int32, (n, 256), 0)
        j = lax.broadcasted_iota(jnp.int32, (n, 256), 1)
        code = r + 1
        for g in range(1, 8):
            code = code + jnp.where(r >= g * slots, 64 - slots, 0)
        at = ((j // 2) % 8) * 64
        number = kept.astype(jnp.int32)
        hits = [jnp.where(at + number[c : c + 1] == code, values[c : c + 1], 0.0) for c in (0, 1)]
        return jnp.sum(hits[0] + hits[1], axis=1, keepdims=True)

    def column(values, n, first):
        r = lax.broadcasted_iota(jnp.int32, (n, 256), 0) + first
        j = lax.broadcasted_iota(jnp.int32, (n, 256), 1)
        at = ((r // 4) % 16) * 16 + (r // 64) * 2 + r % 2
        picked = jnp.where((r // 2) % 2 == 1, values[1:2], values[0:1])
        return jnp.sum(jnp.where(at == j, picked, 0.0), axis=1, keepdims=True)

    slope = (by_slot(weight) * u_ref[...].astype(F32)).astype(BF)
    grad_ref[...] = lax.dot_general(
        x_ref[...], slope, (((0,), (0,)), ((), ())), preferred_element_type=F32
    )
    first = z_ref[0] * 64
    lane = lax.broadcasted_iota(jnp.int32, (64, 128), 1)
    own_ref[...] = jnp.where(lane == 0, column(weight, 64, first), column(excess, 64, first))


def tail(z, mine, got, u_all, x_all):
    vmem = pl.BlockSpec(memory_space=pltpu.VMEM)
    out = (
        jax.ShapeDtypeStruct((x_all.shape[1], u_all.shape[1]), F32),
        jax.ShapeDtypeStruct((64, 128), F32),
    )
    return pl.pallas_call(
        tail_kernel,
        out_shape=out,
        in_specs=[pl.BlockSpec(memory_space=pltpu.SMEM)] + [vmem] * 4,
        out_specs=(vmem, vmem),
        compiler_params=pltpu.CompilerParams(vmem_limit_bytes=16 * 1024 * 1024),
        cost_estimate=pl.CostEstimate(
            flops=2 * x_all.size * u_all.shape[1], bytes_accessed=4 * x_all.size, transcendentals=4096
        ),
    )(z, mine, got, u_all, x_all)


def columns(a, first, size):
    return lax.slice_in_dim(a, first, first + size, axis=a.ndim - 1)


def on_device(
    hidden_ref, head, targets, train_loss, keep_index, layer_input, cotangent, layer_weight
):
    co = coords()
    voc_dev = head.shape[1]
    half = head.shape[0] // 2
    dv = layer_weight.shape[1]
    rows = train_loss.shape[0]
    slots = keep_index.shape[1]
    vocab = lax.axis_index("vocab")
    shard = lax.axis_index("dp") * 32 + vocab

    head = head.T
    other_head = ex(head, "c", 1)

    def bits(axis, b):
        return bit(co, axis, b)

    lane = lax.broadcasted_iota(jnp.int32, (2, 128), 1)
    t = targets[:, None]
    meta = jnp.where(lane == 0, t // 65536, jnp.where(lane == 1, (t // 256) % 256, t % 256))
    meta = jnp.where(lane < 3, meta, 0).astype(BF)
    h = jnp.concatenate([hidden_ref, meta], axis=1)[None]
    h = pair_up(h, ex(h, "z", 4), bits("z", 2), 0)[:, None]
    hot = (keep_index[0][:, None] == jnp.arange(rows, dtype=jnp.int32)[None, :]).astype(BF)
    inputs, cotangent_kept = [
        jnp.dot(hot, full, preferred_element_type=F32).astype(BF) for full in (layer_input, cotangent)
    ]
    xs = lax.ppermute(inputs, AXES, plane_pairs(False))

    h = pair_up(h, ex(h, "z", 2), bits("z", 1), 1)[:, :, None]
    xs = gather_direct(xs, co, "x", 0)
    h, xs = sync(h, xs)

    h = pair_up(h, ex(h, "z", 1), bits("z", 0), 2).reshape(16, 2 * half + 128)
    xs = gather_direct(xs, co, "y", 0).reshape(2, 2, 4, slots, dv)
    xs = jnp.concatenate([xs[:, j].swapaxes(0, 1).reshape(8 * slots, dv) for j in (0, 1)], 1)
    h, xs, other_head = sync(h, xs, other_head)

    p, q = h[:, :half], h[:, half:]
    p = gather_direct(p, co, "y", 0)
    got = ex(xs, "c", 1)
    p, q, xs, got = sync(p, q, xs, got)

    q = gather_direct(q, co, "x", 0)
    low, high = [
        jnp.concatenate([columns(a, 0, dv), columns(b, 0, dv), columns(a, dv, dv), columns(b, dv, dv)], 1)
        for a, b in ((xs, got), (got, xs))
    ]
    x_all = jnp.where(bits("c", 0), high, low)
    pre = jnp.dot(x_all, layer_weight, preferred_element_type=F32)
    p, q, pre = sync(p, q, pre)

    p_near, q_near = ring_first(p, "x"), ring_first(q, "y")
    pre = halve(pre.reshape(2, 2, 2, slots, dv), co, "z", 0, 2, BF)
    pre = halve(pre, co, "z", 1, 1, BF).astype(BF).reshape(2 * slots, dv)
    p_near, q_near, pre = sync(p_near, q_near, pre)

    p_far, q_far = ring_second(*p_near, "x", half // 2), ring_second(*q_near, "y", half // 2)
    got = ex(jnp.concatenate([pre, cotangent_kept]), "z", 4)
    pre = pre.astype(F32) + got[: 2 * slots].astype(F32)
    cot = pair_up(cotangent_kept, got[2 * slots :], bits("z", 2), 0)
    u = (cot.astype(F32) * derivative(pre)).astype(BF)
    p_far, q_far, u = sync(p_far, q_far, u)

    p = ring_stack(p, p_near, p_far, co, "x", 0, half // 2).reshape(256, half)
    q = ring_stack(q, q_near, q_far, co, "y", 1, half // 2).reshape(256, half + 128)
    first = jnp.stack([shard * voc_dev, (shard ^ 1) * voc_dev]).astype(jnp.int32)
    stats, u = sync(local_stats(p, q, head, other_head, first)[:3], u)

    here = jnp.arange(8, dtype=jnp.int32) == co["z"]
    number = jnp.arange(1, slots + 1, dtype=jnp.int32)
    here_kept = keep_index[0][None, :] == jnp.arange(rows, dtype=jnp.int32)[:, None]
    marks = jnp.sum(jnp.where(here_kept, number[None, :], 0), axis=1)
    own = jnp.stack([train_loss, marks.astype(F32)]).reshape(2, 16, 1, 2, 2)
    own = jnp.where(bits("c", 0), own[:, :, :, 1], own[:, :, :, 0])
    own = jnp.where(here[None, None, :, None], own, 0.0).reshape(2, 256)

    u_all = jnp.zeros((2, 4, slots, dv), BF)
    u_all = lax.dynamic_update_slice_in_dim(u_all, u.reshape(2, 1, slots, dv), co["z"] % 4, 1)
    mine = jnp.concatenate([stats, own])
    for mask in (1, 3, 2):
        got_s, got = without_terms(ex(with_terms(mine, u), "z", mask), 5)
        stats, own = combine(stats, got_s[:3]), own + got_s[3:]
        got = got.reshape(2, 1, slots, dv)
        u_all = lax.dynamic_update_slice_in_dim(u_all, got, (co["z"] % 4) ^ mask, 1)
    u_all = u_all.reshape(8 * slots, dv)
    stats, own, u_all = sync(stats, own, u_all)

    terms = lax.dot_general(
        u_all, layer_weight, (((1,), (1,)), ((), ())), preferred_element_type=F32
    ).astype(BF)
    back = jnp.concatenate([columns(terms, j * dv, dv) for j in (0, 2, 1, 3)])
    hi = bits("c", 0)
    keep, send = split_halves(back, hi)
    got_s, got = without_terms(ex(with_terms(jnp.concatenate([stats, own]), send), "c", 1), 5)
    stats, own = [
        jnp.where(hi, jnp.stack([b, a], 1), jnp.stack([a, b], 1)).reshape(-1, 256)
        for a, b in ((stats, got_s[:3]), (own, got_s[3:]))
    ]
    back = (keep.astype(F32) + got.astype(F32)).astype(BF)
    back = back.reshape(2, 4, 2, slots, dv).transpose(2, 0, 1, 3, 4).reshape(4, 4 * slots, dv)
    stats, back = four_way(stats, back, co, "y")
    stats, back = four_way(stats, back.astype(BF).reshape(4, slots, dv), co, "x")
    back = lax.ppermute(back.astype(BF), AXES, plane_pairs(True))
    mine = jnp.concatenate([stats, own])
    got_s = ex(mine, "z", 4)
    spread = lax.dot_general(hot, back, (((0,), (0,)), ((), ())), preferred_element_type=F32)
    mine_grad = cotangent.astype(F32) + spread
    grad_weight, own = tail(co["z"].astype(jnp.int32)[None], mine, got_s, u_all, x_all)
    grad_input = (own[:, :1] * mine_grad).astype(BF)
    return (own[:, 1], grad_weight, grad_input)


def solution(mesh):
    in_specs = (
        P(("dp", "vocab"), None),
        P(None, ("dp", "vocab")),
        P(("dp", "vocab")),
        P("dp"),
        P("dp", None),
        P("dp", "vocab"),
        P("dp", "vocab"),
        P("dp", "vocab"),
    )
    out_specs = (P("dp"), P("dp", "vocab"), P("dp", "vocab"))
    return jax.shard_map(
        on_device, mesh=mesh, in_specs=in_specs, out_specs=out_specs, check_vma=False
    )
```
